32 devices in a mesh: ctx: 8 (over y, x, core), tp: 4 (over z).
Axes of the slice: x: 2, y: 2, z: 4, core: 2. Of those that a mesh axis runs over, the one named last changes fastest.
Arguments:
- queries: bfloat16 [4096, 8192], P('ctx', 'tp'), may hold values from -1.796875 to 1.796875
- keys: bfloat16 [4096, 8192], P('ctx', 'tp'), may hold values from -1.796875 to 1.796875
- values: bfloat16 [4096, 8192], P('ctx', 'tp'), may hold values from -12 to 12
- log_decay: float32 [64, 4096], P('tp', 'ctx'), may hold values from -2 to 0
- gain: float32 [8192], P('tp'), may hold values from 0.1 to 1.9
- grad_out: bfloat16 [4096, 8192], P('ctx', 'tp'), may hold values from -5 to 5
Outputs:
- normed: bfloat16 [4096, 8192], P('ctx', 'tp')
- grad_queries: bfloat16 [4096, 8192], P('ctx', 'tp')
- grad_keys: bfloat16 [4096, 8192], P('ctx', 'tp')
- grad_values: bfloat16 [4096, 8192], P('ctx', 'tp')
The draws below stay inside these ranges and needn't reach their ends.
All inputs are finite; a program needn't handle non-finite values.
Results may differ from the reference program's by a relative error of at most 0.0069.
Values sent between devices are 32-bit elements; how exact they have to be, the bound alone decides.
No kernel may reach another device: no remote copies, remote signals or barrier semaphores. Data moves between devices by JAX's collectives and lax.ppermute only.
A program may use at most 128 MiB of HBM per device.

```python
import math
import jax
import jax.numpy as jnp
from jax import lax

ATTENTION_HEADS = 64
E = 128
BLOCK = 512
SEQUENCE_TOKENS = 4096


def head_rates(key):
    base = jax.random.fold_in(key, 11)
    picked = jax.random.randint(jax.random.fold_in(base, 1), (ATTENTION_HEADS,), 0, 100)
    share = 50
    fast_rate = jnp.exp(jax.random.uniform(jax.random.fold_in(base, 2), (ATTENTION_HEADS,), jnp.float32, math.log(1.0 / 50.0), math.log(1.0 / 30.0)))
    slow_rate = 0.5 * math.log(2.0) / SEQUENCE_TOKENS * jnp.exp(jax.random.uniform(jax.random.fold_in(base, 3), (ATTENTION_HEADS,), jnp.float32, math.log(0.5), 0.0))
    return jnp.where(picked < share, fast_rate, slow_rate)


def draw_log_decay(key, part):
    decay_rates = head_rates(key)
    local = jax.random.fold_in(key, 23)
    decay_factor = jnp.exp(jax.random.uniform(jax.random.fold_in(local, 1), (ATTENTION_HEADS, SEQUENCE_TOKENS), jnp.float32, math.log(0.5), math.log(2.0)))
    position_slots = jax.random.randint(jax.random.fold_in(local, 2), (ATTENTION_HEADS, 3), 0, SEQUENCE_TOKENS)
    retained_fraction = jax.random.uniform(jax.random.fold_in(local, 3), (ATTENTION_HEADS, 3), jnp.float32, 0.6, 0.8)
    token_positions = jnp.arange(SEQUENCE_TOKENS, dtype=jnp.int32)
    decay_windows = jnp.zeros((ATTENTION_HEADS, SEQUENCE_TOKENS), jnp.float32)
    for column_offset in range(3):
        decay_windows = decay_windows + jnp.where(token_positions[None, :] == position_slots[:, column_offset:column_offset + 1], jnp.log(retained_fraction[:, column_offset:column_offset + 1]), 0.0)
    return (-decay_rates[:, None] * decay_factor + decay_windows).astype(jnp.float32)


def draw_values(key, part):
    decay_rates = head_rates(key)
    rising = jnp.power(3.0, jnp.arange(ATTENTION_HEADS, dtype=jnp.float32) / (ATTENTION_HEADS - 1))
    scales = rising * jnp.sqrt(jnp.minimum(1.0, 40.0 * decay_rates))
    noise_key = jax.random.fold_in(key, 31)
    noise = jnp.clip(jax.random.normal(noise_key, (SEQUENCE_TOKENS, ATTENTION_HEADS, E), jnp.float32), -4.0, 4.0)
    return (noise * scales[None, :, None]).reshape(SEQUENCE_TOKENS, ATTENTION_HEADS * E).astype(jnp.bfloat16)


def level_of(rng, extent, shards, low, largest):
    loudness = 1.0
    for position, shards_of in shards:
        steps = jax.random.uniform(jax.random.fold_in(jax.random.fold_in(rng, 6), position), (shards_of,), jnp.float32, low / len(shards), largest / len(shards))
        loudness = loudness * jnp.repeat(jnp.exp(steps), extent[position] // shards_of).reshape((-1,) + (1,) * (len(extent) - 1 - position))
    return loudness


def gaussian(key, dims, deviation, bound, cuts=(), kind=jnp.bfloat16):
    entries = jax.random.normal(key, dims, jnp.float32) * deviation
    if len(cuts) > 0:
        entries = level_of(key, dims, cuts, -0.22, 0.18) * entries
    return jnp.clip(entries, min=-bound, max=bound).astype(kind)


def setup_inputs(seed: int = 0) -> dict:
    key_list = jax.random.split(jax.random.key(seed), 7)
    return {
        "queries": gaussian(key_list[0], (SEQUENCE_TOKENS, ATTENTION_HEADS * E), 0.3, 1.796875, ((0, 8), (1, 4))),
        "keys": gaussian(key_list[1], (SEQUENCE_TOKENS, ATTENTION_HEADS * E), 0.3, 1.796875, ((0, 8), (1, 4))),
        "values": draw_values(jax.random.fold_in(key_list[6], 71), 0),
        "log_decay": draw_log_decay(jax.random.fold_in(key_list[6], 71), 0),
        "gain": jnp.clip(1.0 + 0.18 * jax.random.normal(key_list[4], (ATTENTION_HEADS * E,), jnp.float32), 0.1, 1.9),
        "grad_out": gaussian(key_list[5], (SEQUENCE_TOKENS, ATTENTION_HEADS * E), 1.0, 5.0, ((0, 8), (1, 4))),
    }


def half(matrix):
    return lax.optimization_barrier(matrix.astype(jnp.bfloat16))

def wide(matrix):
    return matrix.astype(jnp.float32)

def prepare(query_blk, key_blk, decay_blk):
    cumulative = jnp.cumsum(decay_blk, axis=1)
    totals = cumulative[:, -1]
    row_pos = lax.broadcasted_iota(jnp.int32, (BLOCK, BLOCK), 0)
    col_pos = lax.broadcasted_iota(jnp.int32, (BLOCK, BLOCK), 1)
    causal = row_pos >= col_pos
    spread = cumulative[:, :, None] - cumulative[:, None, :]
    weights = jnp.exp(jnp.where(causal[None], spread, -1e+30))
    scores = jnp.einsum('the,she->hts', wide(query_blk), wide(key_blk))
    probs = half(scores * weights)
    rise = jnp.exp(cumulative).T[:, :, None]
    fall = jnp.exp(totals[:, None] - cumulative).T[:, :, None]
    query_dec = half(wide(query_blk) * rise)
    key_dec = half(wide(key_blk) * fall)
    return (weights, probs, rise, fall, query_dec, key_dec, jnp.exp(totals))

def reference(queries, keys, values, log_decay, gain, grad_out):
    blocks = SEQUENCE_TOKENS // BLOCK
    shape_four = (blocks, BLOCK, ATTENTION_HEADS, E)
    query_all = queries.reshape(shape_four)
    key_all = keys.reshape(shape_four)
    value_all = values.reshape(shape_four)
    decay_all = log_decay.reshape(ATTENTION_HEADS, blocks, BLOCK).transpose(1, 0, 2)

    def forward_step(state, pieces):
        query_blk, key_blk, value_blk, decay_blk = pieces
        weights, probs, rise, fall, query_dec, key_dec, decay_factor = prepare(query_blk, key_blk, decay_blk)
        state_half = half(state)
        attended = jnp.einsum('hts,she->the', wide(probs), wide(value_blk)) + jnp.einsum('the,hef->thf', wide(query_dec), wide(state_half))
        contrib = jnp.einsum('she,shf->hef', wide(key_dec), wide(value_blk))
        return (decay_factor[:, None, None] * state + contrib, (attended, state))
    start_state = jnp.zeros((ATTENTION_HEADS, E, E), jnp.float32)
    final_state, outputs = lax.scan(forward_step, start_state, (query_all, key_all, value_all, decay_all))
    attended, entering = outputs
    attended = attended.reshape(SEQUENCE_TOKENS, ATTENTION_HEADS * E)
    squares = lax.optimization_barrier(jnp.sum(attended * attended, axis=1))
    inverse = lax.rsqrt(squares / (ATTENTION_HEADS * E) + 1e-05)
    normed = (gain[None, :] * attended * inverse[:, None]).astype(jnp.bfloat16)
    scaled_grad = gain[None, :] * grad_out.astype(jnp.float32)
    crossed = lax.optimization_barrier(jnp.sum(scaled_grad * attended, axis=1))
    d_attended = (inverse[:, None] * scaled_grad - attended * (inverse ** 3 * crossed / (ATTENTION_HEADS * E))[:, None]).astype(jnp.bfloat16)
    grad_all = d_attended.reshape(shape_four)

    def backward_step(outflow, pieces):
        query_blk, key_blk, value_blk, decay_blk, grad_blk, state = pieces
        weights, probs, rise, fall, query_dec, key_dec, decay_factor = prepare(query_blk, key_blk, decay_blk)
        d_prob = jnp.einsum('the,she->hts', wide(grad_blk), wide(value_blk))
        d_scores = half(d_prob * weights)
        leave_half = half(outflow)
        state_half = half(state)
        grad_q = jnp.einsum('hts,she->the', wide(d_scores), wide(key_blk)) + rise * jnp.einsum('thf,hef->the', wide(grad_blk), wide(state_half))
        grad_k = jnp.einsum('hts,the->she', wide(d_scores), wide(query_blk)) + fall * jnp.einsum('shf,hef->she', wide(value_blk), wide(leave_half))
        grad_v = jnp.einsum('hts,the->she', wide(probs), wide(grad_blk)) + jnp.einsum('she,hef->shf', wide(key_dec), wide(leave_half))
        state_grad = jnp.einsum('the,thf->hef', wide(query_dec), wide(grad_blk))
        return (decay_factor[:, None, None] * outflow + state_grad, (grad_q, grad_k, grad_v))
    end_grad = jnp.zeros((ATTENTION_HEADS, E, E), jnp.float32)
    first_grad, grads = lax.scan(backward_step, end_grad, (query_all, key_all, value_all, decay_all, grad_all, entering), reverse=True)
    grad_q, grad_k, grad_v = grads
    return (normed, grad_q.reshape(SEQUENCE_TOKENS, ATTENTION_HEADS * E).astype(jnp.bfloat16), grad_k.reshape(SEQUENCE_TOKENS, ATTENTION_HEADS * E).astype(jnp.bfloat16), grad_v.reshape(SEQUENCE_TOKENS, ATTENTION_HEADS * E).astype(jnp.bfloat16))
```

```python
import functools

import jax
import jax.numpy as jnp
from jax import lax
from jax.experimental import pallas as pl
from jax.experimental.pallas import tpu as pltpu
from jax.sharding import PartitionSpec as P

E = 128
BLOCK = 512
CHUNK = 256
CHUNKS = BLOCK // CHUNK
EPSILON = 1e-05
PARTS = 2

F32 = jnp.float32
BF16 = jnp.bfloat16
IN_VMEM = pl.BlockSpec(memory_space=pltpu.VMEM)
ANY = pl.BlockSpec(memory_space=pl.ANY)
MIB = 1 << 20


def call(kernel, outs, *args, flops=0, anywhere=(), after=(), outs_anywhere=0, scratch=(), alias=None, limit=8):
    args = (*args, *after)
    skip = len(after)

    def body(*refs):
        kept = len(args) - skip
        kernel(*refs[:kept], *refs[len(args) :])

    in_specs = [IN_VMEM] * (len(args) - skip) + [ANY] * skip
    for operand in anywhere:
        in_specs[operand] = ANY
    return pl.pallas_call(
        body,
        out_shape=[
            jax.ShapeDtypeStruct(shape, dtype) if n < outs_anywhere else pltpu.VMEM(shape, dtype)
            for n, (shape, dtype) in enumerate(outs)
        ],
        in_specs=in_specs,
        out_specs=[ANY] * outs_anywhere + [IN_VMEM] * (len(outs) - outs_anywhere),
        scratch_shapes=scratch,
        input_output_aliases=alias or {},
        compiler_params=pltpu.CompilerParams(vmem_limit_bytes=limit * MIB),
        cost_estimate=pl.CostEstimate(flops=flops, bytes_accessed=0, transcendentals=0),
    )(*args)


def dot(a, b, contract):
    return lax.dot_general(a, b, ((contract[:1], contract[1:]), ((), ())), preferred_element_type=F32)


def span(i, n=1):
    return slice(i * E, (i + n) * E)


def chunk(c):
    return slice(c * CHUNK, (c + 1) * CHUNK)


def bits(reverse=False):
    me = lax.axis_index("ctx")
    if reverse:
        me = 7 - me
    return me & 1, (me >> 1) & 1, me >> 2


def columns(half, i, n=1):
    if half is None:
        return span(i, n)
    core = lax.axis_index("ctx") & 1
    base = core if i < half else 1 - core
    return pl.ds(pl.multiple_of(base * (half * E) + (i % half) * E, E), n * E)


def head_rows(half, i, n):
    core = lax.axis_index("ctx") & 1
    base = core if i < half else 1 - core
    return pl.ds(pl.multiple_of(base * half, half), n)


def contribution(half, index, keys, values, fall_row, factor, contrib, early):
    for n, i in enumerate(index):
        cols = columns(half, i)
        dec = (keys[:, cols].T.astype(F32) * fall_row[i : i + 1, :]).astype(BF16)
        v = values[:, cols]
        total = None
        for c in range(CHUNKS):
            new = dot(dec[:, chunk(c)], v[chunk(c)], (1, 0))
            if c > 0:
                total = factor[c][i : i + 1, :] * total + new
            else:
                total = new
            if c < CHUNKS - 1:
                early[span(n), :] = total
        contrib[span(n), :] = total


def start_kernel(half, order, first, heads, log_decay, keys, values, cum_row, rise_row, fall_row, factor, k_out, v_out, contrib, early, rows, sems):
    rows[...] = jnp.zeros_like(rows)
    moves = []
    if half is None:
        moves.append(pltpu.make_async_copy(log_decay, rows.at[0:heads, :], sems.at[0]))
    else:
        for n, i in enumerate((0, half)):
            source = log_decay.at[head_rows(half, i, half), :]
            moves.append(pltpu.make_async_copy(source, rows.at[i : i + half, :], sems.at[n]))
    for move in moves:
        move.start()
    pieces = []
    for n, (i, count) in enumerate(order):
        cols = columns(half, i, count)
        pieces.append(
            [
                pltpu.make_async_copy(keys.at[:, cols], k_out.at[:, cols], sems.at[2 + 2 * n]),
                pltpu.make_async_copy(values.at[:, cols], v_out.at[:, cols], sems.at[3 + 2 * n]),
            ]
        )
        for move in pieces[-1]:
            move.start()
    up_to = (
        lax.broadcasted_iota(jnp.int32, (CHUNK, CHUNK), 0)
        <= lax.broadcasted_iota(jnp.int32, (CHUNK, CHUNK), 1)
    ).astype(F32).astype(BF16)
    for move in moves:
        move.wait()
    for c in range(CHUNKS):
        whole = rows[:, chunk(c)]
        high = whole.astype(BF16)
        rest = whole - high.astype(F32)
        middle = rest.astype(BF16)
        low = (rest - middle.astype(F32)).astype(BF16)
        cum = (dot(low, up_to, (1, 0)) + dot(middle, up_to, (1, 0))) + dot(high, up_to, (1, 0))
        total = cum[:, CHUNK - 1 : CHUNK]
        cum_row[:, chunk(c)] = cum
        rise_row[:, chunk(c)] = jnp.exp(cum)
        fall_row[:, chunk(c)] = jnp.exp(total - cum)
        factor[c] = jnp.broadcast_to(jnp.exp(total), (total.shape[0], E))
    whole = factor[0]
    for c in range(1, CHUNKS):
        whole = whole * factor[c]
    factor[CHUNKS] = whole
    for move in pieces[0]:
        move.wait()
    contribution(half, first, k_out, v_out, fall_row, factor, contrib, early)
    for piece in pieces[1:]:
        for move in piece:
            move.wait()


def contrib_kernel(half, index, keys, values, fall_row, factor, contrib, early):
    contribution(half, index, keys, values, fall_row, factor, contrib, early)


def column_kernel(cum_row, cum_col, rise_col, fall_col, rows):
    rows[...] = jnp.zeros_like(rows)
    rows[0 : cum_row.shape[0], :] = cum_row[...]
    col = rows[...].T
    cum_col[...] = col
    rise_col[...] = jnp.exp(col)
    for c in range(CHUNKS):
        fall_col[chunk(c), :] = jnp.exp(col[(c + 1) * CHUNK - 1 : (c + 1) * CHUNK, :] - col[chunk(c)])


def chip_kernel(count, reverse, kept, got, own_factor, other_factor, *sums):
    lower = bits(reverse)[0] == 0
    for n in range(len(sums) * count):
        mine = jnp.where(lower, other_factor[n : n + 1, :], 1.0)
        theirs = jnp.where(lower, 1.0, own_factor[n : n + 1, :])
        sums[n // count][span(n % count), :] = mine * kept[span(n), :] + theirs * got[span(n), :]


def second_kernel(reverse, got_x, own_x, got_y, own_y, factor, factor_x, factor_d, send_y, send_x):
    _, x, y = bits(reverse)
    right, later = x == 1, y == 1
    count = got_x.shape[0] // E
    for n in range(count):
        f, fx = factor[n : n + 1, :], factor_x[n : n + 1, :]
        p = jnp.where(right, f, 1.0)
        q = jnp.where(right, 1.0, fx)
        send_y[span(n), :] = p * got_x[span(n), :] + q * own_x[span(n), :]
        n2 = count + n
        f, fd = factor[n2 : n2 + 1, :], factor_d[n2 : n2 + 1, :]
        p = jnp.where(later, jnp.where(right, 1.0, f * fd), 0.0)
        q = jnp.where(later, jnp.where(right, 0.0, jnp.ones_like(f)), 1.0)
        send_x[span(n), :] = p * got_y[span(n), :] + q * own_y[span(n), :]


def enter_kernel(reverse, one_x, two_y, one_y, two_x, factor_x, factor_d, own_factor, other_factor, kept, got, mine, send):
    core, x, y = bits(reverse)
    lower, right, later = core == 0, x == 1, y == 1
    count = one_x.shape[0] // E
    for n in range(2 * count):
        fx, fd = factor_x[n : n + 1, :], factor_d[n : n + 1, :]
        one = jnp.ones_like(fx)
        if n < count:
            first, second = one_x[span(n), :], two_y[span(n), :]
            w = jnp.where(right, one, 0.0)
            u = jnp.where(later, jnp.where(right, fx, 1.0), 0.0)
        else:
            first, second = one_y[span(n - count), :], two_x[span(n - count), :]
            w = jnp.where(later, jnp.where(right, fx, fd), 0.0)
            u = jnp.where(later, one, jnp.where(right, one, 0.0))
        low = w * first + u * second
        f = jnp.where(lower, own_factor[n : n + 1, :], other_factor[n : n + 1, :])
        high = f * low + jnp.where(lower, kept[span(n), :], got[span(n), :])
        mine[span(n), :] = jnp.where(lower, low, high)
        send[span(n), :] = jnp.where(lower, high, low)


def intra_kernel(half, index, queries, keys, values, cum_row, rise_row, cum_col, rise_col, fall_col, intra, query_dec, query_dec_t, key_dec, value_dec):
    causal = lax.broadcasted_iota(jnp.int32, (CHUNK, CHUNK), 0) >= lax.broadcasted_iota(
        jnp.int32, (CHUNK, CHUNK), 1
    )
    for n, i in enumerate(index):
        cols = columns(half, i)
        q, k, v = queries[:, cols], keys[:, cols], values[:, cols]
        rise, fall = rise_col[:, i : i + 1], fall_col[:, i : i + 1]
        query_dec[:, span(n)] = (q.astype(F32) * rise).astype(BF16)
        query_dec_t[span(n), :] = (q.T.astype(F32) * rise_row[i : i + 1, :]).astype(BF16)
        key_dec[:, span(n)] = (k.astype(F32) * fall).astype(BF16)
        value_dec[:, span(n)] = (v.astype(F32) * fall).astype(BF16)
        for c in range(CHUNKS):
            at = chunk(c)
            spread = cum_col[at, i : i + 1] - cum_row[i : i + 1, at]
            weight = jnp.exp(jnp.where(causal, spread, -1e30))
            probs = (dot(q[at], k[at], (1, 1)) * weight).astype(BF16)
            intra[at, span(n)] = dot(probs, v[at], (1, 0))


def attend_kernel(half, index, query_dec, intra, entering, early, factor, grad_out, gain, *refs):
    if len(refs) == 6:
        total, cross = refs[0][...], refs[1][...]
    else:
        total = cross = jnp.zeros((BLOCK, E), F32)
    attended, state, squares, crossed = refs[-4:]
    totals, crosses = [], []
    for c in range(CHUNKS):
        at = chunk(c)
        totals.append(total[at])
        crosses.append(cross[at])
    for n, i in enumerate(index):
        cols = columns(half, i)
        now = entering[span(n), :]
        for c in range(CHUNKS):
            at = chunk(c)
            if c > 0:
                now = factor[0, i : i + 1, :] * now + early[span(n), :]
            rounded = now.astype(BF16)
            state[c, span(n), :] = rounded
            out = intra[at, span(n)] + dot(query_dec[at, span(n)], rounded, (1, 0))
            attended[at, span(n)] = out
            totals[c] += out * out
            crosses[c] += (gain[:, cols] * grad_out[at, cols].astype(F32)) * out
    for c in range(CHUNKS):
        squares[chunk(c), :] = totals[c]
        crossed[chunk(c), :] = crosses[c]


def sum_kernel(squares, crossed, sums):
    ones = jnp.ones((8, E), F32)

    def row(x):
        return lax.dot_general(
            ones, x, (((1,), (1,)), ((), ())), precision=lax.Precision.HIGHEST, preferred_element_type=F32
        )

    first = lax.broadcasted_iota(jnp.int32, (8, BLOCK), 0) == 0
    sums[...] = jnp.where(first, row(squares[...]), row(crossed[...]))


def scale_kernel(features, ours, theirs, inverse, coefficient):
    sums = ours[...] + theirs[...]
    inv = lax.rsqrt(sums[0:1, :] / features + EPSILON)
    coef = inv * inv * inv * sums[1:2, :] / features
    inverse[...] = jnp.broadcast_to(inv, (E, BLOCK)).T
    coefficient[...] = jnp.broadcast_to(coef, (E, BLOCK)).T


def outer_kernel(half, index, inverse, coefficient, attended, query_dec_t, factor, grad_out, gain, d_attended, flow, late):
    for n, i in enumerate(index):
        cols = columns(half, i)
        total = None
        for c in reversed(range(CHUNKS)):
            at = chunk(c)
            scaled = gain[:, cols] * grad_out[at, cols].astype(F32)
            grad = (inverse[at] * scaled - attended[at, span(n)] * coefficient[at]).astype(BF16)
            d_attended[at, span(n)] = grad
            new = dot(query_dec_t[span(n), at], grad, (1, 0))
            total = new if total is None else factor[c, i : i + 1, :] * total + new
            if c > 0:
                late[span(n), :] = total
        flow[span(n), :] = total


def copies(staged, outs, sems, n, cols):
    made = []
    for m, out in enumerate(outs):
        copy = pltpu.make_async_copy(staged.at[m, n], out.at[:, cols], sems.at[m, n])
        copy.start()
        made.append(copy)
    return made


def back_kernel(half, index, queries, keys, values, cum_row, cum_col, rise_col, d_attended, state, attended, inverse, gain, *refs):
    normed, grad_q, intra_k, intra_v, staged, sems = refs[-6:]
    causal = lax.broadcasted_iota(jnp.int32, (CHUNK, CHUNK), 0) <= lax.broadcasted_iota(
        jnp.int32, (CHUNK, CHUNK), 1
    )
    made = []
    for n, i in enumerate(index):
        cols = columns(half, i)
        q, k, v, grad = queries[:, cols], keys[:, cols], values[:, cols], d_attended[:, span(n)]
        staged[0, n] = (gain[:, cols] * attended[:, span(n)] * inverse[...]).astype(BF16)
        for c in range(CHUNKS):
            at = chunk(c)
            spread = cum_row[i : i + 1, at] - cum_col[at, i : i + 1]
            weight = jnp.exp(jnp.where(causal, spread, -1e30))
            probs = (dot(k[at], q[at], (1, 1)) * weight).astype(BF16)
            d_scores = (dot(v[at], grad[at], (1, 1)) * weight).astype(BF16)
            intra_v[at, span(n)] = dot(probs, grad[at], (1, 0))
            intra_k[at, span(n)] = dot(d_scores, q[at], (1, 0))
            staged[1, n, at, :] = (
                dot(d_scores, k[at], (0, 0))
                + rise_col[at, i : i + 1] * dot(grad[at], state[c, span(n), :], (1, 1))
            ).astype(BF16)
        made += copies(staged, (normed, grad_q), sems, n, cols)
    for copy in made:
        copy.wait()


def leave_kernel(half, index, value_dec, key_dec, intra_k, intra_v, leaving, late, factor, *refs):
    grad_k, grad_v, staged, sems = refs[-4:]
    made = []
    for n, i in enumerate(index):
        cols = columns(half, i)
        now = leaving[span(n), :]
        for c in reversed(range(CHUNKS)):
            at = chunk(c)
            if c < CHUNKS - 1:
                now = factor[c + 1, i : i + 1, :] * now + late[span(n), :]
            rounded = now.astype(BF16)
            staged[0, n, at, :] = (
                intra_k[at, span(n)] + dot(value_dec[at, span(n)], rounded, (1, 1))
            ).astype(BF16)
            staged[1, n, at, :] = (
                intra_v[at, span(n)] + dot(key_dec[at, span(n)], rounded, (1, 0))
            ).astype(BF16)
        made += copies(staged, (grad_k, grad_v), sems, n, cols)
    for copy in made:
        copy.wait()


def exchange(x, axis, bit):
    return lax.ppermute(x, axis, [(i, i ^ bit) for i in range(lax.axis_size(axis))])


def gathered(contrib, factor, reverse):
    devices, place = lax.axis_size("ctx"), lax.axis_index("ctx")
    all_contrib = lax.all_gather(contrib, "ctx")
    all_factor = lax.all_gather(factor, "ctx")

    def lap(step, state):
        at = devices - 1 - step if reverse else step
        reached = at > place if reverse else at < place
        new = (all_factor[at][:, None, :] * state.reshape(-1, E, E)).reshape(-1, E) + all_contrib[at]
        return jnp.where(reached, new, state)

    return lax.fori_loop(0, devices, lap, jnp.zeros_like(contrib))


def summed(x):
    devices = lax.axis_size("tp")
    if devices == 1 or devices & (devices - 1):
        return lax.psum(x, "tp"), jnp.zeros_like(x)
    bit = 1
    while True:
        other = exchange(x, "tp", bit)
        bit *= 2
        if bit == devices:
            return x, other
        x = x + other


def per_device(queries, keys, values, log_decay, gain, grad_out):
    heads, tokens = log_decay.shape
    assert tokens == BLOCK and CHUNKS == 2
    features = heads * E * lax.axis_size("tp")
    fast = lax.axis_size("ctx") == 8 and heads % 16 == 0
    half = heads // 2 if fast else None
    parts = PARTS if fast else 1
    own = (half or heads) // parts
    group = own // 2
    gain = gain[None, :]
    product = 2 * BLOCK * E * E
    rows = max(16, heads)

    pieces = [(p, side) for p in range(parts) for side in ((1, 0) if fast else (0,))]
    index = {(p, side): [side * (half or 0) + p * own + i for i in range(own)] for p, side in pieces}
    order = [(index[piece][0], own) for piece in pieces]
    tall, flat, wide = (own * E, E), (BLOCK, own * E), (BLOCK, E)

    cum_row, rise_row, fall_row, factor, keys, values, contrib, early = call(
        functools.partial(start_kernel, half, order, index[pieces[0]], heads),
        [((rows, BLOCK), F32)] * 3 + [((CHUNKS + 1, rows, E), F32)] + [(keys.shape, BF16)] * 2 + [(tall, F32)] * 2,
        log_decay, keys, values, anywhere=(0, 1, 2),
        scratch=[pltpu.VMEM((rows, BLOCK), F32), pltpu.SemaphoreType.DMA((2 + 2 * len(order),))],
        flops=4 * product,
    )
    whole_factor = factor[CHUNKS]
    contribs, earlies = {pieces[0]: contrib}, {pieces[0]: early}
    if fast:
        other_factor = exchange(whole_factor, "ctx", 1)[half:]
        own_factor = whole_factor[:half]
        chip_factor = own_factor * other_factor

    def at(p):
        return slice(p * own, (p + 1) * own)

    def first_step(reverse, kept, got, p):
        for_x, for_y = call(
            functools.partial(chip_kernel, group, reverse),
            [((group * E, E), F32)] * 2,
            kept, got, own_factor[at(p)], other_factor[at(p)],
        )
        return kept, got, for_x, for_y, exchange(for_x, "ctx", 2), exchange(for_y, "ctx", 4)

    def second_step(reverse, p, step, after):
        kept, got, for_x, for_y, got_x, got_y = step
        send_y, send_x = call(
            functools.partial(second_kernel, reverse), [((group * E, E), F32)] * 2,
            got_x, for_x, got_y, for_y, chip_factor[at(p)], factor_x[at(p)], factor_d[at(p)], after=after,
        )
        return *step, exchange(send_y, "ctx", 4), exchange(send_x, "ctx", 2)

    def last_step(reverse, p, step, after):
        kept, got, for_x, for_y, got_x, got_y, two_y, two_x = step
        enter, send = call(
            functools.partial(enter_kernel, reverse), [(tall, F32)] * 2,
            got_x, two_y, got_y, two_x, factor_x[at(p)], factor_d[at(p)], own_factor[at(p)], other_factor[at(p)], kept, got,
            after=after,
        )
        return {(p, 0): enter, (p, 1): exchange(send, "ctx", 1)}

    def contribute(piece, after):
        contribs[piece], earlies[piece] = call(
            functools.partial(contrib_kernel, half, index[piece]), [(tall, F32)] * 2,
            keys, values, fall_row, factor, flops=product * own, after=after,
        )

    steps, last = [], ()
    if fast:
        for p in range(parts):
            if p:
                contribute((p, 1), last)
            got = exchange(contribs[p, 1], "ctx", 1)
            contribute((p, 0), last)
            steps.append(first_step(False, contribs[p, 0], got, p))
            last = (steps[-1][2],)
        chip_factor, _ = lax.optimization_barrier((chip_factor, last[0]))
        factor_x = exchange(chip_factor, "ctx", 2)
        factor_d = exchange(chip_factor, "ctx", 6)

    cum_col, rise_col, fall_col = call(
        column_kernel, [(wide, F32)] * 3, cum_row, scratch=[pltpu.VMEM((E, BLOCK), F32)], after=last
    )
    intra, query_dec, query_dec_t, key_dec, value_dec = {}, {}, {}, {}, {}
    for piece in pieces:
        intra[piece], query_dec[piece], query_dec_t[piece], key_dec[piece], value_dec[piece] = call(
            functools.partial(intra_kernel, half, index[piece]),
            [(flat, F32), (flat, BF16), ((own * E, BLOCK), BF16), (flat, BF16), (flat, BF16)],
            queries, keys, values, cum_row, rise_row, cum_col, rise_col, fall_col, flops=own * 8 * product, after=last,
        )
    entering = {}
    if fast:
        for p in range(parts):
            steps[p] = second_step(False, p, steps[p], (intra[pieces[p]],))
        for p in range(parts):
            entering |= last_step(False, p, steps[p], (intra[pieces[parts + p]],))
    else:
        entering[pieces[0]] = gathered(contribs[pieces[0]], whole_factor[:heads], False)

    attended, state, sums = {}, {}, []
    for p in range(parts):
        for side in (0, 1) if fast else (0,):
            piece = p, side
            attended[piece], state[piece], *sums = call(
                functools.partial(attend_kernel, half, index[piece]),
                [(flat, F32), ((CHUNKS, *tall), BF16), (wide, F32), (wide, F32)],
                query_dec[piece], intra[piece], entering[piece], earlies[piece], factor, grad_out, gain, *sums,
                flops=own * product,
            )
    (sums,) = call(sum_kernel, [((8, BLOCK), F32)], *sums)
    inverse, coefficient = call(functools.partial(scale_kernel, features), [(wide, F32)] * 2, *summed(sums))

    d_attended, flow, late = {}, {}, {}

    def outer(piece, after):
        d_attended[piece], flow[piece], late[piece] = call(
            functools.partial(outer_kernel, half, index[piece]), [(flat, BF16), (tall, F32), (tall, F32)],
            inverse, coefficient, attended[piece], query_dec_t[piece], factor, grad_out, gain,
            flops=product * own, after=after,
        )

    steps, last = [], ()
    if fast:
        for p in range(parts):
            outer((p, 1), last)
            got = exchange(flow[p, 1], "ctx", 1)
            outer((p, 0), last)
            steps.append(first_step(True, flow[p, 0], got, p))
            last = (steps[-1][2],)
    else:
        outer(pieces[0], ())

    full = (queries.shape, BF16)
    staging = [pltpu.VMEM((2, own, BLOCK, E), BF16), pltpu.SemaphoreType.DMA((2, own))]
    results, intra_k, intra_v = [], {}, {}
    for piece in pieces:
        args = [
            queries, keys, values, cum_row, cum_col, rise_col,
            d_attended[piece], state[piece], attended[piece], inverse, gain, *results,
        ]
        where = (len(args) - 2, len(args) - 1) if results else ()
        *results, intra_k[piece], intra_v[piece] = call(
            functools.partial(back_kernel, half, index[piece]),
            [full, full, (flat, F32), (flat, F32)],
            *args, flops=own * 20 * product, anywhere=where, alias=dict(zip(where, (0, 1))), outs_anywhere=2,
            scratch=staging, after=last,
        )
    normed, grad_q = results

    leaving = {}
    if fast:
        for p in range(parts):
            steps[p] = second_step(True, p, steps[p], (intra_k[pieces[p]],))
        for p in range(parts):
            leaving |= last_step(True, p, steps[p], (intra_k[pieces[parts + p]],))
    else:
        leaving[pieces[0]] = gathered(flow[pieces[0]], whole_factor[:heads], True)

    results = []
    for p in range(parts):
        for side in (0, 1) if fast else (0,):
            piece = p, side
            args = [
                value_dec[piece], key_dec[piece], intra_k[piece], intra_v[piece],
                leaving[piece], late[piece], factor, *results,
            ]
            where = (len(args) - 2, len(args) - 1) if results else ()
            results = call(
                functools.partial(leave_kernel, half, index[piece]), [full, full],
                *args, flops=2 * own * product, anywhere=where, alias=dict(zip(where, (0, 1))), outs_anywhere=2,
                scratch=staging,
            )
    return normed, grad_q, *results


def solution(mesh):
    in_specs = (
        P("ctx", "tp"),
        P("ctx", "tp"),
        P("ctx", "tp"),
        P("tp", "ctx"),
        P("tp"),
        P("ctx", "tp"),
    )
    out_specs = (P("ctx", "tp"),) * 4
    return jax.shard_map(
        per_device, mesh=mesh, in_specs=in_specs, out_specs=out_specs, check_vma=False
    )
```

```python
import functools

import jax
import jax.numpy as jnp
from jax import lax
from jax.experimental import pallas as pl
from jax.experimental.pallas import tpu as pltpu
from jax.sharding import PartitionSpec as P

E = 128
BLOCK = 512
CHUNK = 256
CHUNKS = BLOCK // CHUNK
EPSILON = 1e-05
GROUPS = 2

F32 = jnp.float32
BF16 = jnp.bfloat16
IN_VMEM = pl.BlockSpec(memory_space=pltpu.VMEM)
IN_HBM = pl.BlockSpec(memory_space=pltpu.HBM)
ANY = pl.BlockSpec(memory_space=pl.ANY)
MIB = 1 << 20


def call(kernel, outs, *args, anywhere=(), after=(), outs_anywhere=0, scratch=(), alias=None, limit=20):
    args = [pltpu.with_memory_space_constraint(x, pltpu.HBM) if n in anywhere else x for n, x in enumerate(args)]
    args += after
    skip = len(after)

    def body(*refs):
        kept = len(args) - skip
        kernel(*refs[:kept], *refs[len(args) :])

    in_specs = [IN_VMEM] * (len(args) - skip) + [ANY] * skip
    for operand in anywhere:
        in_specs[operand] = IN_HBM
    return pl.pallas_call(
        body,
        out_shape=[
            (pltpu.HBM if n < outs_anywhere else pltpu.VMEM)(shape, dtype) for n, (shape, dtype) in enumerate(outs)
        ],
        in_specs=in_specs,
        out_specs=[IN_HBM] * outs_anywhere + [IN_VMEM] * (len(outs) - outs_anywhere),
        scratch_shapes=scratch,
        input_output_aliases=alias or {},
        compiler_params=pltpu.CompilerParams(vmem_limit_bytes=limit * MIB),
        cost_estimate=pl.CostEstimate(flops=0, bytes_accessed=0, transcendentals=0),
    )(*args)


def dot(a, b, contract):
    return lax.dot_general(a, b, ((contract[:1], contract[1:]), ((), ())), preferred_element_type=F32)


def beside_copies(compute):
    pl.when(lax.axis_index("ctx") >= 0)(compute)


def span(i, n=1):
    return slice(i * E, (i + n) * E)


def chunk(c):
    return slice(c * CHUNK, (c + 1) * CHUNK)


def bits(reverse=False):
    me = lax.axis_index("ctx")
    if reverse:
        me = 7 - me
    return me & 1, (me >> 1) & 1, me >> 2


def columns(half, i, n=1):
    if half is None:
        return span(i, n)
    core = lax.axis_index("ctx") & 1
    base = core if i < half else 1 - core
    return pl.ds(pl.multiple_of(base * (half * E) + (i % half) * E, E), n * E)


def head_rows(half, i, n):
    core = lax.axis_index("ctx") & 1
    base = core if i < half else 1 - core
    return pl.ds(pl.multiple_of(base * half, half), n)


def contribution(index, keys, values, fall_row, factor, contrib, early):
    decayed = []
    for n, i in enumerate(index):
        turned = keys[:, span(n)].T.astype(F32)
        decayed.append((turned * fall_row[i : i + 1, :]).astype(BF16))
    news = [
        [dot(dec[:, chunk(c)], values[chunk(c), span(n)], (1, 0)) for c in range(CHUNKS)]
        for n, dec in enumerate(decayed)
    ]
    for n, i in enumerate(index):
        early[span(n), :] = news[n][0]
        contrib[span(n), :] = factor[1, i : i + 1, :] * news[n][0] + news[n][1]


def fetch(half, pieces, sources, outs, sems):
    made = []
    for m, index in enumerate(pieces):
        cols = columns(half, index[0], len(index))
        made.append([])
        for n, source in enumerate(sources):
            k = m * len(sources) + n
            made[-1].append(pltpu.make_async_copy(source.at[:, cols], outs[k], sems.at[k]))
            made[-1][-1].start()
    return made


def start_kernel(half, pieces, heads, log_decay, gain, keys, values, *refs):
    cum_row, rise_row, fall_row, factor, gain_out = refs[:5]
    rows, sems, more = refs[-3:]
    brought, (contrib, early) = refs[5:-5], refs[-5:-3]
    rows[...] = jnp.zeros_like(rows)
    moves = [pltpu.make_async_copy(gain, gain_out, more.at[2])]
    if half is None:
        moves.append(pltpu.make_async_copy(log_decay, rows.at[0:heads, :], more.at[0]))
    else:
        for n, i in enumerate((0, half)):
            source = log_decay.at[head_rows(half, i, half), :]
            moves.append(pltpu.make_async_copy(source, rows.at[i : i + half, :], more.at[n]))
    for move in moves:
        move.start()
    made = fetch(half, pieces, (keys, values), brought, sems)
    for move in moves:
        move.wait()
    @beside_copies
    def _():
        up_to = (
            lax.broadcasted_iota(jnp.int32, (CHUNK, CHUNK), 0)
            <= lax.broadcasted_iota(jnp.int32, (CHUNK, CHUNK), 1)
        ).astype(F32).astype(BF16)
        for c in range(CHUNKS):
            whole = rows[:, chunk(c)]
            high = whole.astype(BF16)
            rest = whole - high.astype(F32)
            middle = rest.astype(BF16)
            low = (rest - middle.astype(F32)).astype(BF16)
            cum = (dot(low, up_to, (1, 0)) + dot(middle, up_to, (1, 0))) + dot(high, up_to, (1, 0))
            total = cum[:, CHUNK - 1 : CHUNK]
            cum_row[:, chunk(c)] = cum
            rise_row[:, chunk(c)] = jnp.exp(cum)
            fall_row[:, chunk(c)] = jnp.exp(total - cum)
            factor[c] = jnp.broadcast_to(jnp.exp(total), (total.shape[0], E))
        whole = factor[0] * factor[1]
        factor[CHUNKS] = whole
        if half is not None:
            contrib[len(pieces[0]) * E :, :] = factor[CHUNKS, half : 2 * half]

    for move in made[0]:
        move.wait()
    beside_copies(functools.partial(contribution, pieces[0], *brought[:2], fall_row, factor, contrib, early))
    for moves in made[1:]:
        for move in moves:
            move.wait()


def contrib_kernel(index, keys, values, fall_row, factor, contrib, early):
    contribution(index, keys, values, fall_row, factor, contrib, early)


def column_kernel(cum_row, cum_col, rise_col, fall_col, rows):
    rows[...] = jnp.zeros_like(rows)
    rows[0 : cum_row.shape[0], :] = cum_row[...]
    col = rows[...].T
    cum_col[...] = col
    rise_col[...] = jnp.exp(col)
    for c in range(CHUNKS):
        fall_col[chunk(c), :] = jnp.exp(col[(c + 1) * CHUNK - 1 : (c + 1) * CHUNK, :] - col[chunk(c)])


def chip_kernel(count, reverse, kept, got, own_factor, other_factor, sums):
    if sums.shape[0] > count * E:
        sums[count * E :, :] = own_factor[...] * other_factor[...]
    lower = bits(reverse)[0] == 0
    for n in range(count):
        mine = jnp.where(lower, other_factor[n : n + 1, :], 1.0)
        theirs = jnp.where(lower, 1.0, own_factor[n : n + 1, :])
        sums[span(n), :] = mine * kept[span(n), :] + theirs * got[span(n), :]


def second_kernel(count, group, reverse, one, own, factor, factor_x, factor_d, send):
    _, x, y = bits(reverse)
    right, later = x == 1, y == 1
    for n in range(count):
        f, fx, fd = factor[n : n + 1, :], factor_x[n : n + 1, :], factor_d[n : n + 1, :]
        if group == 0:
            p = jnp.where(right, f, 1.0)
            q = jnp.where(right, 1.0, fx)
        else:
            p = jnp.where(later, jnp.where(right, 1.0, f * fd), 0.0)
            q = jnp.where(later, jnp.where(right, 0.0, jnp.ones_like(f)), 1.0)
        send[span(n), :] = p * one[span(n), :] + q * own[span(n), :]


def enter_kernel(count, group, reverse, one, two, factor_x, factor_d, own_factor, other_factor, kept, got, mine, send):
    core, x, y = bits(reverse)
    lower, right, later = core == 0, x == 1, y == 1
    for n in range(count):
        fx, fd = factor_x[n : n + 1, :], factor_d[n : n + 1, :]
        ones = jnp.ones_like(fx)
        if group == 0:
            w = jnp.where(right, ones, 0.0)
            u = jnp.where(later, jnp.where(right, fx, 1.0), 0.0)
        else:
            w = jnp.where(later, jnp.where(right, fx, fd), 0.0)
            u = jnp.where(later, ones, jnp.where(right, ones, 0.0))
        low = w * one[span(n), :] + u * two[span(n), :]
        f = jnp.where(lower, own_factor[n : n + 1, :], other_factor[n : n + 1, :])
        high = f * low + jnp.where(lower, kept[span(n), :], got[span(n), :])
        mine[span(n), :] = jnp.where(lower, low, high)
        send[span(n), :] = jnp.where(lower, high, low)


def intra_kernel(half, index, grad_out, queries, keys, values, cum_row, rise_row, cum_col, rise_col, fall_col, *refs):
    intra, query_dec, query_dec_t, key_dec, value_dec, grad_here, sems = refs
    made = fetch(half, [index], (grad_out,), (grad_here,), sems)
    @beside_copies
    def _():
        causal = lax.broadcasted_iota(jnp.int32, (CHUNK, CHUNK), 0) >= lax.broadcasted_iota(
            jnp.int32, (CHUNK, CHUNK), 1
        )
        scores, probs = [], []
        for n, i in enumerate(index):
            cols = columns(half, i)
            for c in range(CHUNKS):
                scores.append((n, i, c, dot(queries[chunk(c), cols], keys[chunk(c), span(n)], (1, 1))))
        for n, i, c, score in scores:
            at = chunk(c)
            spread = cum_col[at, i : i + 1] - cum_row[i : i + 1, at]
            weight = jnp.exp(jnp.where(causal, spread, -1e30))
            probs.append((n, i, c, (score * weight).astype(BF16)))
        for n, i, c, prob in probs:
            intra[chunk(c), span(n)] = dot(prob, values[chunk(c), span(n)], (1, 0))
        for n, i in enumerate(index):
            cols = columns(half, i)
            rise, fall = rise_col[:, i : i + 1], fall_col[:, i : i + 1]
            query_dec[:, span(n)] = (queries[:, cols].astype(F32) * rise).astype(BF16)
            query_dec_t[span(n), :] = (queries[:, cols].T.astype(F32) * rise_row[i : i + 1, :]).astype(BF16)
            key_dec[:, span(n)] = (keys[:, span(n)].astype(F32) * fall).astype(BF16)
            value_dec[:, span(n)] = (values[:, span(n)].astype(F32) * fall).astype(BF16)

    made[0][0].wait()


def attend_kernel(half, index, query_dec, intra, entering, early, factor, grad_out, gain, *refs):
    attended, state, squares, crossed = refs[-4:]
    states, inters = [], []
    for n, i in enumerate(index):
        now = entering[span(n), :]
        states.append((n, 0, now.astype(BF16)))
        states.append((n, 1, (factor[0, i : i + 1, :] * now + early[span(n), :]).astype(BF16)))
    for n, c, rounded in states:
        state[c, span(n), :] = rounded
        inters.append((n, c, dot(query_dec[chunk(c), span(n)], rounded, (1, 0))))
    totals, crosses = [0.0] * CHUNKS, [0.0] * CHUNKS
    for n, c, inter in inters:
        at, cols = chunk(c), columns(half, index[n])
        out = intra[at, span(n)] + inter
        attended[at, span(n)] = out
        totals[c] += out * out
        crosses[c] += (gain[:, cols] * grad_out[at, span(n)].astype(F32)) * out
    for c in range(CHUNKS):
        at = chunk(c)
        if len(refs) == 6:
            totals[c], crosses[c] = totals[c] + refs[0][at], crosses[c] + refs[1][at]
        squares[at, :] = totals[c]
        crossed[at, :] = crosses[c]


def sum_kernel(squares, crossed, sums):
    square = jnp.sum(squares[...].T, axis=0, keepdims=True)
    cross = jnp.sum(crossed[...].T, axis=0, keepdims=True)
    first = lax.broadcasted_iota(jnp.int32, (8, BLOCK), 0) == 0
    sums[...] = jnp.where(first, square, cross)


def scale_kernel(features, ours, theirs, inverse, coefficient):
    sums = ours[...] + theirs[...]
    inv = lax.rsqrt(sums[0:1, :] / features + EPSILON)
    coef = inv * inv * inv * sums[1:2, :] / features
    inverse[...] = jnp.broadcast_to(inv, (E, BLOCK)).T
    coefficient[...] = jnp.broadcast_to(coef, (E, BLOCK)).T


def outer_kernel(half, index, inverse, coefficient, attended, query_dec_t, factor, grad_out, gain, d_attended, flow, late):
    grads, news = [], []
    for n, i in enumerate(index):
        cols = columns(half, i)
        for c in range(CHUNKS):
            at = chunk(c)
            scaled = gain[:, cols] * grad_out[at, span(n)].astype(F32)
            grads.append((n, c, (inverse[at] * scaled - attended[at, span(n)] * coefficient[at]).astype(BF16)))
    for n, c, grad in grads:
        d_attended[chunk(c), span(n)] = grad
        news.append(dot(query_dec_t[span(n), chunk(c)], grad, (1, 0)))
    for n, i in enumerate(index):
        first, second = news[CHUNKS * n : CHUNKS * (n + 1)]
        late[span(n), :] = second
        flow[span(n), :] = factor[0, i : i + 1, :] * second + first


def flush(staged, outs, sems, half, index):
    made = []
    for m, out in enumerate(outs):
        cols = columns(half, index[0], len(index))
        made.append(pltpu.make_async_copy(staged.at[m], out.at[:, cols], sems.at[m]))
        made[-1].start()
    return made


def back_kernel(half, index, before, queries, keys, values, cum_row, cum_col, rise_col, d_attended, state, attended, inverse, gain, *refs):
    made = []
    if before is not None:
        made = flush(refs[0], refs[-6:-4], refs[-1], half, before)
    intra_k, intra_v, staged = refs[-4:-1]
    @beside_copies
    def _():
        causal = lax.broadcasted_iota(jnp.int32, (CHUNK, CHUNK), 0) <= lax.broadcasted_iota(
            jnp.int32, (CHUNK, CHUNK), 1
        )
        products, rounded = [], []
        for n, i in enumerate(index):
            cols = columns(half, i)
            for c in range(CHUNKS):
                at = chunk(c)
                grad = d_attended[at, span(n)]
                score = dot(keys[at, span(n)], queries[at, cols], (1, 1))
                d_prob = dot(values[at, span(n)], grad, (1, 1))
                products.append((n, i, c, score, d_prob, dot(grad, state[c, span(n), :], (1, 1))))
        for n, i, c, score, d_prob, inter in products:
            at = chunk(c)
            spread = cum_row[i : i + 1, at] - cum_col[at, i : i + 1]
            weight = jnp.exp(jnp.where(causal, spread, -1e30))
            rounded.append((n, i, c, (score * weight).astype(BF16), (d_prob * weight).astype(BF16), inter))
        for n, i, c, prob, d_score, inter in rounded:
            at, cols = chunk(c), columns(half, i)
            intra_v[at, span(n)] = dot(prob, d_attended[at, span(n)], (1, 0))
            intra_k[at, span(n)] = dot(d_score, queries[at, cols], (1, 0))
            staged[1, at, span(n)] = (dot(d_score, keys[at, span(n)], (0, 0)) + rise_col[at, i : i + 1] * inter).astype(BF16)
        for n, i in enumerate(index):
            staged[0, :, span(n)] = (gain[:, columns(half, i)] * attended[:, span(n)] * inverse[...]).astype(BF16)

    for copy in made:
        copy.wait()


def leave_kernel(half, index, before, last, split, value_dec, key_dec, intra_k, intra_v, leaving, late, factor, *refs):
    staged, sems, out_sems = refs[-3:]
    made = []
    if before is not None:
        made = flush(refs[0], refs[-7:-5] if split else refs[-5:-3], sems, half, before)
    @beside_copies
    def _():
        flows, products = [], []
        for n, i in enumerate(index):
            now = leaving[span(n), :]
            flows.append((n, 1, now.astype(BF16)))
            flows.append((n, 0, (factor[1, i : i + 1, :] * now + late[span(n), :]).astype(BF16)))
        for n, c, flow in flows:
            at = chunk(c)
            products.append((n, c, dot(value_dec[at, span(n)], flow, (1, 1)), dot(key_dec[at, span(n)], flow, (1, 0))))
        for n, c, of_key, of_value in products:
            at = chunk(c)
            staged[0, at, span(n)] = (intra_k[at, span(n)] + of_key).astype(BF16)
            staged[1, at, span(n)] = (intra_v[at, span(n)] + of_value).astype(BF16)

    if last:
        made += flush(staged, refs[-5:-3], out_sems, half, index)
    for copy in made:
        copy.wait()


def exchange(x, axis, bit):
    return lax.ppermute(x, axis, [(i, i ^ bit) for i in range(lax.axis_size(axis))])


def gathered(contrib, factor, reverse):
    devices, place = lax.axis_size("ctx"), lax.axis_index("ctx")
    all_contrib = lax.all_gather(contrib, "ctx")
    all_factor = lax.all_gather(factor, "ctx")

    def lap(step, state):
        at = devices - 1 - step if reverse else step
        reached = at > place if reverse else at < place
        new = (all_factor[at][:, None, :] * state.reshape(-1, E, E)).reshape(-1, E) + all_contrib[at]
        return jnp.where(reached, new, state)

    return lax.fori_loop(0, devices, lap, jnp.zeros_like(contrib))


def summed(x):
    devices = lax.axis_size("tp")
    if devices == 1 or devices & (devices - 1):
        return lax.psum(x, "tp"), jnp.zeros_like(x)
    bit = 1
    while True:
        other = exchange(x, "tp", bit)
        bit *= 2
        if bit == devices:
            return x, other
        x = x + other


def per_device(queries, keys, values, log_decay, gain, grad_out):
    heads, tokens = log_decay.shape
    assert tokens == BLOCK and CHUNKS == 2
    features = heads * E * lax.axis_size("tp")
    fast = lax.axis_size("ctx") == 8 and heads % 16 == 0
    half = heads // 2 if fast else None
    groups = GROUPS if fast else 1
    own = (half or heads) // groups
    gain = gain[None, :]
    rows = max(16, heads)

    sides = (1, 0) if fast else (0,)
    pieces = [(g, side) for g in range(groups) for side in sides]
    late_pieces = [(g, side) for g in range(groups) for side in reversed(sides)]
    index = {(g, side): [side * (half or 0) + g * own + i for i in range(own)] for g, side in pieces}
    tall, flat, wide = (own * E, E), (BLOCK, own * E), (BLOCK, E)
    staged_shape = ((2, BLOCK, own * E), BF16)
    bits_of = {0: (2, 4), 1: (4, 2)}

    def at(g):
        return slice(g * own, (g + 1) * own)

    n = len(pieces)
    cum_row, rise_row, fall_row, factor, gain, *made = call(
        functools.partial(start_kernel, half, [index[piece] for piece in pieces], heads),
        [((rows, BLOCK), F32)] * 3 + [((CHUNKS + 1, rows, E), F32), (gain.shape, F32)]
        + [(flat, BF16)] * (2 * n) + [((own * E + (half or 0), E), F32), (tall, F32)],
        log_decay, gain, keys, values, anywhere=(0, 1, 2, 3),
        scratch=[pltpu.VMEM((rows, BLOCK), F32), pltpu.SemaphoreType.DMA((2 * n,)), pltpu.SemaphoreType.DMA((3,))],
    )
    whole_factor = factor[CHUNKS]
    key, value = {}, {}
    for m, piece in enumerate(pieces):
        key[piece], value[piece] = made[2 * m : 2 * m + 2]
    contrib, early = {pieces[0]: made[-2]}, {pieces[0]: made[-1]}

    def contribute(piece):
        contrib[piece], early[piece] = call(
            functools.partial(contrib_kernel, index[piece]), [(tall, F32)] * 2,
            key[piece], value[piece], fall_row, factor,
        )

    def first_step(reverse, kept, got, g, after=()):
        more = half if g == 0 and not reverse else 0
        f, h = (own_factor, other_factor) if more else (own_factor[at(g)], other_factor[at(g)])
        (chip,) = call(
            functools.partial(chip_kernel, own, reverse), [((own * E + more, E), F32)], kept, got, f, h, after=after
        )
        return kept, got, chip, exchange(chip, "ctx", bits_of[g][0])

    def second_step(reverse, g, step, after):
        kept, got, chip, one = step
        (send,) = call(
            functools.partial(second_kernel, own, g, reverse), [(tall, F32)],
            one, chip, chip_factor[at(g)], factor_x[at(g)], (factor_d if g else factor_x)[at(g)], after=after,
        )
        return *step, exchange(send, "ctx", bits_of[g][1])

    def last_step(reverse, g, step, after):
        kept, got, chip, one, two = step
        enter, send = call(
            functools.partial(enter_kernel, own, g, reverse), [(tall, F32)] * 2,
            one, two, factor_x[at(g)], (factor_d if g else factor_x)[at(g)], own_factor[at(g)], other_factor[at(g)], kept, got,
            after=after,
        )
        return {(g, 0): enter, (g, 1): exchange(send, "ctx", 1)}

    steps, last = [], ()
    if fast:
        gots = [exchange(contrib[0, 1], "ctx", 1)]
        contribute((0, 0))
        for g in range(1, groups):
            contribute((g, 1))
            gots.append(exchange(contrib[g, 1], "ctx", 1))
        own_factor, other_factor = whole_factor[:half], gots[0][own * E : own * E + half]
        for g in range(groups):
            if g:
                contribute((g, 0))
            steps.append(first_step(False, contrib[g, 0], gots[g], g, [contrib[groups - 1, 1]]))
        chip_factor = steps[0][2][own * E :]
        factor_x = steps[0][3][own * E :]
        factor_d = exchange(chip_factor, "ctx", 6)
        last = [step[2] for step in steps]

    cum_col, rise_col, fall_col = call(
        column_kernel, [(wide, F32)] * 3, cum_row, scratch=[pltpu.VMEM((E, BLOCK), F32)], after=last
    )
    intra, query_dec, query_dec_t, key_dec, value_dec, grad_here = {}, {}, {}, {}, {}, {}
    for piece in pieces:
        made = call(
            functools.partial(intra_kernel, half, index[piece]),
            [(flat, F32), (flat, BF16), ((own * E, BLOCK), BF16)] + [(flat, BF16)] * 3,
            grad_out, queries, key[piece], value[piece], cum_row, rise_row, cum_col, rise_col, fall_col, after=last, anywhere=(0,), scratch=[pltpu.SemaphoreType.DMA((1,))],
        )
        intra[piece], query_dec[piece], query_dec_t[piece], key_dec[piece], value_dec[piece], grad_here[piece] = made
    attended, state, sums = {}, {}, []

    def attend(piece, sums):
        attended[piece], state[piece], *sums = call(
            functools.partial(attend_kernel, half, index[piece]),
            [(flat, F32), ((CHUNKS, *tall), BF16), (wide, F32), (wide, F32)],
            query_dec[piece], intra[piece], entering[piece], early[piece], factor, grad_here[piece], gain, *sums,
        )
        return sums

    entering = {}
    if fast:
        for g in range(groups):
            steps[g] = second_step(False, g, steps[g], [intra[pieces[g]], intra[pieces[1]]])
        for g in range(groups):
            entering |= last_step(False, g, steps[g], [intra[pieces[-1]], intra[pieces[-2]], *sums])
            if g == 0:
                sums = attend((0, 0), sums)
    else:
        entering[pieces[0]] = gathered(contrib[pieces[0]], whole_factor[:heads], False)
    for piece in late_pieces:
        if piece not in attended:
            sums = attend(piece, sums)
    (sums,) = call(sum_kernel, [((8, BLOCK), F32)], *sums)
    inverse, coefficient = call(functools.partial(scale_kernel, features), [(wide, F32)] * 2, *summed(sums))

    d_attended, flow, late = {}, {}, {}

    def outer(piece, after):
        d_attended[piece], flow[piece], late[piece] = call(
            functools.partial(outer_kernel, half, index[piece]), [(flat, BF16), (tall, F32), (tall, F32)],
            inverse, coefficient, attended[piece], query_dec_t[piece], factor, grad_here[piece], gain, after=after,
        )

    steps, last = [], ()
    outer(pieces[0], ())
    if fast:
        gots = [exchange(flow[0, 1], "ctx", 1)]
        outer((0, 0), ())
        for g in range(1, groups):
            outer((g, 1), ())
            gots.append(exchange(flow[g, 1], "ctx", 1))
        for g in range(groups):
            if g:
                outer((g, 0), ())
            steps.append(first_step(True, flow[g, 0], gots[g], g, [flow[groups - 1, 1]]))
        last = [step[2] for step in steps]

    full = (queries.shape, BF16)
    sems = pltpu.SemaphoreType.DMA((2,))
    results, before, staged, intra_k, intra_v = [], None, [], {}, {}
    for piece in pieces:
        args = [
            queries, key[piece], value[piece], cum_row, cum_col, rise_col,
            d_attended[piece], state[piece], attended[piece], inverse, gain, *staged, *results,
        ]
        where = (len(args) - 2, len(args) - 1) if results else ()
        *results, intra_k[piece], intra_v[piece], out = call(
            functools.partial(back_kernel, half, index[piece], before),
            [full] * 2 + [(flat, F32)] * 2 + [staged_shape],
            *args, anywhere=where, alias=dict(zip(where, (0, 1))), outs_anywhere=2,
            scratch=[sems], after=last,
        )
        before, staged = index[piece], [out]

    leaving, others = {}, []

    def leave(piece, before, staged, results, others):
        last = piece in late_pieces[-2:]
        first = piece == late_pieces[0]
        split = first and last
        held = results if first else others
        args = [
            value_dec[piece], key_dec[piece], intra_k[piece], intra_v[piece],
            leaving[piece], late[piece], factor, *staged, *held,
        ]
        where = (len(args) - 2, len(args) - 1) if held else ()
        outs = 4 if split else 2
        made = call(
            functools.partial(leave_kernel, half, index[piece], before, last, split),
            [full] * outs + [staged_shape] * (not last),
            *args, anywhere=where, alias=dict(zip(where, (0, 1))), outs_anywhere=outs,
            scratch=[pltpu.VMEM(*staged_shape)] * last + [sems, sems],
        )
        out = None if last else made[-1]
        made = made[:outs]
        if first:
            results, others = made[:2], made[2:]
        else:
            others = made
        return (None, [], results, others) if last else (index[piece], [out], results, others)

    carried = (before, staged, results, others)
    if fast:
        for g in range(groups):
            steps[g] = second_step(True, g, steps[g], [intra_k[pieces[1]]])
        for g in range(groups):
            leaving |= last_step(True, g, steps[g], [intra_k[pieces[-1]], *carried[1]])
            if g == 0:
                carried = leave((0, 0), *carried)
    else:
        leaving[pieces[0]] = gathered(flow[pieces[0]], whole_factor[:heads], True)
    for n, piece in enumerate(late_pieces):
        if n or not fast:
            carried = leave(piece, *carried)
    return *carried[2], *carried[3]


def solution(mesh):
    in_specs = (
        P("ctx", "tp"),
        P("ctx", "tp"),
        P("ctx", "tp"),
        P("tp", "ctx"),
        P("tp"),
        P("ctx", "tp"),
    )
    out_specs = (P("ctx", "tp"),) * 4
    return jax.shard_map(
        per_device, mesh=mesh, in_specs=in_specs, out_specs=out_specs, check_vma=False
    )
```

```python
import functools

import jax
import jax.numpy as jnp
from jax import lax
from jax.experimental import pallas as pl
from jax.experimental.pallas import tpu as pltpu
from jax.sharding import PartitionSpec as P

E = 128
BLOCK = 512
CHUNK = 256
CHUNKS = BLOCK // CHUNK
EPSILON = 1e-05
GROUPS = 2

F32 = jnp.float32
BF16 = jnp.bfloat16
IN_VMEM = pl.BlockSpec(memory_space=pltpu.VMEM)
IN_HBM = pl.BlockSpec(memory_space=pltpu.HBM)
ANY = pl.BlockSpec(memory_space=pl.ANY)
MIB = 1 << 20


def call(kernel, outs, *args, anywhere=(), after=(), outs_anywhere=0, scratch=(), alias=None, limit=20):
    args = [pltpu.with_memory_space_constraint(x, pltpu.HBM) if n in anywhere else x for n, x in enumerate(args)]
    args += after
    skip = len(after)

    def body(*refs):
        kept = len(args) - skip
        kernel(*refs[:kept], *refs[len(args) :])

    in_specs = [IN_VMEM] * (len(args) - skip) + [ANY] * skip
    for operand in anywhere:
        in_specs[operand] = IN_HBM
    return pl.pallas_call(
        body,
        out_shape=[
            (pltpu.HBM if n < outs_anywhere else pltpu.VMEM)(shape, dtype) for n, (shape, dtype) in enumerate(outs)
        ],
        in_specs=in_specs,
        out_specs=[IN_HBM] * outs_anywhere + [IN_VMEM] * (len(outs) - outs_anywhere),
        scratch_shapes=scratch,
        input_output_aliases=alias or {},
        compiler_params=pltpu.CompilerParams(vmem_limit_bytes=limit * MIB),
        cost_estimate=pl.CostEstimate(flops=0, bytes_accessed=0, transcendentals=0),
    )(*args)


def dot(a, b, contract):
    return lax.dot_general(a, b, ((contract[:1], contract[1:]), ((), ())), preferred_element_type=F32)


def beside_copies(compute):
    pl.when(lax.axis_index("ctx") >= 0)(compute)


def span(i, n=1):
    return slice(i * E, (i + n) * E)


def chunk(c):
    return slice(c * CHUNK, (c + 1) * CHUNK)


def bits(reverse=False):
    me = lax.axis_index("ctx")
    if reverse:
        me = 7 - me
    return me & 1, (me >> 1) & 1, me >> 2


def columns(half, i, n=1):
    if half is None:
        return span(i, n)
    core = lax.axis_index("ctx") & 1
    base = core if i < half else 1 - core
    return pl.ds(pl.multiple_of(base * (half * E) + (i % half) * E, E), n * E)


def head_rows(half, i, n):
    core = lax.axis_index("ctx") & 1
    base = core if i < half else 1 - core
    return pl.ds(pl.multiple_of(base * half, half), n)


def contribution(index, keys, values, fall_row, factor, contrib, early):
    decayed = []
    for n, i in enumerate(index):
        turned = keys[:, span(n)].T.astype(F32)
        decayed.append((turned * fall_row[i : i + 1, :]).astype(BF16))
    news = [
        [dot(dec[:, chunk(c)], values[chunk(c), span(n)], (1, 0)) for c in range(CHUNKS)]
        for n, dec in enumerate(decayed)
    ]
    for n, i in enumerate(index):
        early[span(n), :] = news[n][0]
        contrib[span(n), :] = factor[1, i : i + 1, :] * news[n][0] + news[n][1]


def fetch(half, pieces, sources, outs, sems):
    made = []
    for m, index in enumerate(pieces):
        cols = columns(half, index[0], len(index))
        made.append([])
        for n, source in enumerate(sources):
            k = m * len(sources) + n
            made[-1].append(pltpu.make_async_copy(source.at[:, cols], outs[k], sems.at[k]))
            made[-1][-1].start()
    return made


def start_kernel(half, pieces, heads, log_decay, gain, keys, values, *refs):
    cum_row, rise_row, fall_row, factor, gain_out = refs[:5]
    rows, sems, more = refs[-3:]
    brought, (contrib, early) = refs[5:-5], refs[-5:-3]
    rows[...] = jnp.zeros_like(rows)
    moves = [pltpu.make_async_copy(gain, gain_out, more.at[2])]
    if half is None:
        moves.append(pltpu.make_async_copy(log_decay, rows.at[0:heads, :], more.at[0]))
    else:
        for n, i in enumerate((0, half)):
            source = log_decay.at[head_rows(half, i, half), :]
            moves.append(pltpu.make_async_copy(source, rows.at[i : i + half, :], more.at[n]))
    for move in moves:
        move.start()
    made = fetch(half, pieces, (keys, values), brought, sems)
    for move in moves:
        move.wait()
    @beside_copies
    def _():
        up_to = (
            lax.broadcasted_iota(jnp.int32, (CHUNK, CHUNK), 0)
            <= lax.broadcasted_iota(jnp.int32, (CHUNK, CHUNK), 1)
        ).astype(F32).astype(BF16)
        for c in range(CHUNKS):
            whole = rows[:, chunk(c)]
            high = whole.astype(BF16)
            rest = whole - high.astype(F32)
            middle = rest.astype(BF16)
            low = (rest - middle.astype(F32)).astype(BF16)
            cum = (dot(low, up_to, (1, 0)) + dot(middle, up_to, (1, 0))) + dot(high, up_to, (1, 0))
            total = cum[:, CHUNK - 1 : CHUNK]
            cum_row[:, chunk(c)] = cum
            rise_row[:, chunk(c)] = jnp.exp(cum)
            fall_row[:, chunk(c)] = jnp.exp(total - cum)
            factor[c] = jnp.broadcast_to(jnp.exp(total), (total.shape[0], E))
        whole = factor[0] * factor[1]
        factor[CHUNKS] = whole
        if half is not None:
            contrib[len(pieces[0]) * E :, :] = factor[CHUNKS, half : 2 * half]

    for move in made[0]:
        move.wait()
    beside_copies(functools.partial(contribution, pieces[0], *brought[:2], fall_row, factor, contrib, early))
    for moves in made[1:]:
        for move in moves:
            move.wait()


def contrib_kernel(index, keys, values, fall_row, factor, contrib, early):
    contribution(index, keys, values, fall_row, factor, contrib, early)


def column_kernel(cum_row, cum_col, rise_col, fall_col, rows):
    rows[...] = jnp.zeros_like(rows)
    rows[0 : cum_row.shape[0], :] = cum_row[...]
    col = rows[...].T
    cum_col[...] = col
    rise_col[...] = jnp.exp(col)
    for c in range(CHUNKS):
        fall_col[chunk(c), :] = jnp.exp(col[(c + 1) * CHUNK - 1 : (c + 1) * CHUNK, :] - col[chunk(c)])


def chip_kernel(count, reverse, kept, got, own_factor, other_factor, sums):
    if sums.shape[0] > count * E:
        sums[count * E :, :] = own_factor[...] * other_factor[...]
    lower = bits(reverse)[0] == 0
    for n in range(count):
        mine = jnp.where(lower, other_factor[n : n + 1, :], 1.0)
        theirs = jnp.where(lower, 1.0, own_factor[n : n + 1, :])
        sums[span(n), :] = mine * kept[span(n), :] + theirs * got[span(n), :]


def second_kernel(count, group, reverse, one, own, factor, factor_x, factor_d, send):
    _, x, y = bits(reverse)
    over_x, right, later = (bits()[0] if group is None else group) == 0, x == 1, y == 1
    for n in range(count):
        f, fx, fd = factor[n : n + 1, :], factor_x[n : n + 1, :], factor_d[n : n + 1, :]
        ones = jnp.ones_like(f)
        p = jnp.where(over_x, jnp.where(right, f, 1.0), jnp.where(later, jnp.where(right, 1.0, f * fd), 0.0))
        q = jnp.where(over_x, jnp.where(right, 1.0, fx), jnp.where(later, jnp.where(right, 0.0, ones), 1.0))
        send[span(n), :] = p * one[span(n), :] + q * own[span(n), :]


def enter_kernel(count, group, reverse, one, two, factor_x, factor_d, own_factor, other_factor, kept, got, mine, send):
    core, x, y = bits(reverse)
    over_x, lower, right, later = (bits()[0] if group is None else group) == 0, core == 0, x == 1, y == 1
    for n in range(count):
        fx, fd = factor_x[n : n + 1, :], factor_d[n : n + 1, :]
        ones = jnp.ones_like(fx)
        w = jnp.where(over_x, jnp.where(right, ones, 0.0), jnp.where(later, jnp.where(right, fx, fd), 0.0))
        u = jnp.where(
            over_x,
            jnp.where(later, jnp.where(right, fx, 1.0), 0.0),
            jnp.where(later, ones, jnp.where(right, ones, 0.0)),
        )
        low = w * one[span(n), :] + u * two[span(n), :]
        f = jnp.where(lower, own_factor[n : n + 1, :], other_factor[n : n + 1, :])
        high = f * low + jnp.where(lower, kept[span(n), :], got[span(n), :])
        mine[span(n), :] = jnp.where(lower, low, high)
        send[span(n), :] = jnp.where(lower, high, low)


def intra_kernel(half, index, grad_out, queries, keys, values, cum_row, rise_row, cum_col, rise_col, fall_col, *refs):
    intra, query_dec, query_dec_t, key_dec, value_dec, grad_here, sems = refs
    made = fetch(half, [index], (grad_out,), (grad_here,), sems)
    @beside_copies
    def _():
        causal = lax.broadcasted_iota(jnp.int32, (CHUNK, CHUNK), 0) >= lax.broadcasted_iota(
            jnp.int32, (CHUNK, CHUNK), 1
        )
        scores, probs = [], []
        for n, i in enumerate(index):
            cols = columns(half, i)
            for c in range(CHUNKS):
                scores.append((n, i, c, dot(queries[chunk(c), cols], keys[chunk(c), span(n)], (1, 1))))
        for n, i, c, score in scores:
            at = chunk(c)
            spread = cum_col[at, i : i + 1] - cum_row[i : i + 1, at]
            weight = jnp.exp(jnp.where(causal, spread, -1e30))
            probs.append((n, i, c, (score * weight).astype(BF16)))
        for n, i, c, prob in probs:
            intra[chunk(c), span(n)] = dot(prob, values[chunk(c), span(n)], (1, 0))
        for n, i in enumerate(index):
            cols = columns(half, i)
            rise, fall = rise_col[:, i : i + 1], fall_col[:, i : i + 1]
            query_dec[:, span(n)] = (queries[:, cols].astype(F32) * rise).astype(BF16)
            query_dec_t[span(n), :] = (queries[:, cols].T.astype(F32) * rise_row[i : i + 1, :]).astype(BF16)
            key_dec[:, span(n)] = (keys[:, span(n)].astype(F32) * fall).astype(BF16)
            value_dec[:, span(n)] = (values[:, span(n)].astype(F32) * fall).astype(BF16)

    made[0][0].wait()


def attend_kernel(half, index, query_dec, intra, entering, early, factor, grad_out, gain, *refs):
    attended, state, squares, crossed = refs[-4:]
    states, inters = [], []
    for n, i in enumerate(index):
        now = entering[span(n), :]
        states.append((n, 0, now.astype(BF16)))
        states.append((n, 1, (factor[0, i : i + 1, :] * now + early[span(n), :]).astype(BF16)))
    for n, c, rounded in states:
        state[c, span(n), :] = rounded
        inters.append((n, c, dot(query_dec[chunk(c), span(n)], rounded, (1, 0))))
    totals, crosses = [0.0] * CHUNKS, [0.0] * CHUNKS
    for n, c, inter in inters:
        at, cols = chunk(c), columns(half, index[n])
        out = intra[at, span(n)] + inter
        attended[at, span(n)] = out
        totals[c] += out * out
        crosses[c] += (gain[:, cols] * grad_out[at, span(n)].astype(F32)) * out
    for c in range(CHUNKS):
        at = chunk(c)
        if len(refs) == 6:
            totals[c], crosses[c] = totals[c] + refs[0][at], crosses[c] + refs[1][at]
        squares[at, :] = totals[c]
        crossed[at, :] = crosses[c]


def sum_kernel(squares, crossed, sums):
    square = jnp.sum(squares[...].T, axis=0, keepdims=True)
    cross = jnp.sum(crossed[...].T, axis=0, keepdims=True)
    for n in range(BLOCK // E):
        sums[n : n + 1, :] = square[:, span(n)]
        sums[n + 4 : n + 5, :] = cross[:, span(n)]


def scale_kernel(features, ours, theirs, inverse, coefficient):
    sums = ours[...] + theirs[...]
    inv = lax.rsqrt(sums[0:4, :] / features + EPSILON)
    coef = inv * inv * inv * sums[4:8, :] / features
    for n in range(BLOCK // E):
        inverse[span(n), :] = jnp.broadcast_to(inv[n : n + 1, :], (E, E)).T
        coefficient[span(n), :] = jnp.broadcast_to(coef[n : n + 1, :], (E, E)).T


def outer_kernel(half, index, inverse, coefficient, attended, query_dec_t, factor, grad_out, gain, d_attended, flow, late):
    grads, news = [], []
    for n, i in enumerate(index):
        cols = columns(half, i)
        for c in range(CHUNKS):
            at = chunk(c)
            scaled = gain[:, cols] * grad_out[at, span(n)].astype(F32)
            grads.append((n, c, (inverse[at] * scaled - attended[at, span(n)] * coefficient[at]).astype(BF16)))
    for n, c, grad in grads:
        d_attended[chunk(c), span(n)] = grad
        news.append(dot(query_dec_t[span(n), chunk(c)], grad, (1, 0)))
    for n, i in enumerate(index):
        first, second = news[CHUNKS * n : CHUNKS * (n + 1)]
        late[span(n), :] = second
        flow[span(n), :] = factor[0, i : i + 1, :] * second + first


def flush(staged, outs, sems, half, index):
    made = []
    for m, out in enumerate(outs):
        cols = columns(half, index[0], len(index))
        made.append(pltpu.make_async_copy(staged.at[m], out.at[:, cols], sems.at[m]))
        made[-1].start()
    return made


def back_kernel(half, index, before, queries, keys, values, cum_row, cum_col, rise_col, d_attended, state, attended, inverse, gain, *refs):
    made = []
    if before is not None:
        made = flush(refs[0], refs[-6:-4], refs[-1], half, before)
    intra_k, intra_v, staged = refs[-4:-1]
    @beside_copies
    def _():
        causal = lax.broadcasted_iota(jnp.int32, (CHUNK, CHUNK), 0) <= lax.broadcasted_iota(
            jnp.int32, (CHUNK, CHUNK), 1
        )
        products, rounded = [], []
        for n, i in enumerate(index):
            cols = columns(half, i)
            for c in range(CHUNKS):
                at = chunk(c)
                grad = d_attended[at, span(n)]
                score = dot(keys[at, span(n)], queries[at, cols], (1, 1))
                d_prob = dot(values[at, span(n)], grad, (1, 1))
                products.append((n, i, c, score, d_prob, dot(grad, state[c, span(n), :], (1, 1))))
        for n, i, c, score, d_prob, inter in products:
            at = chunk(c)
            spread = cum_row[i : i + 1, at] - cum_col[at, i : i + 1]
            weight = jnp.exp(jnp.where(causal, spread, -1e30))
            rounded.append((n, i, c, (score * weight).astype(BF16), (d_prob * weight).astype(BF16), inter))
        for n, i, c, prob, d_score, inter in rounded:
            at, cols = chunk(c), columns(half, i)
            intra_v[at, span(n)] = dot(prob, d_attended[at, span(n)], (1, 0))
            intra_k[at, span(n)] = dot(d_score, queries[at, cols], (1, 0))
            staged[1, at, span(n)] = (dot(d_score, keys[at, span(n)], (0, 0)) + rise_col[at, i : i + 1] * inter).astype(BF16)
        for n, i in enumerate(index):
            staged[0, :, span(n)] = (gain[:, columns(half, i)] * attended[:, span(n)] * inverse[...]).astype(BF16)

    for copy in made:
        copy.wait()


def leave_part(index, start, value_dec, key_dec, intra_k, intra_v, leaving, late, factor, staged):
    flows, products = [], []
    for n, i in enumerate(index, start):
        now = leaving[span(n), :]
        flows.append((n, 1, now.astype(BF16)))
        flows.append((n, 0, (factor[1, i : i + 1, :] * now + late[span(n), :]).astype(BF16)))
    for n, c, flow in flows:
        at = chunk(c)
        products.append((n, c, dot(value_dec[at, span(n)], flow, (1, 1)), dot(key_dec[at, span(n)], flow, (1, 0))))
    for n, c, of_key, of_value in products:
        at = chunk(c)
        staged[0, at, span(n)] = (intra_k[at, span(n)] + of_key).astype(BF16)
        staged[1, at, span(n)] = (intra_v[at, span(n)] + of_value).astype(BF16)


def leave_kernel(half, before, parts, last, counts, factor, *refs):
    held, aliased, targets = counts
    sources, refs = refs[: 6 * len(parts)], refs[6 * len(parts) :]
    outs = refs[held + aliased : held + aliased + targets]
    staged, sems = refs[-1 - len(parts) : -1], refs[-1]
    if not last:
        staged = (*staged[1:], staged[0])
    made = flush(refs[0], outs[:2], sems.at[0], half, before) if held else []
    for n, index in enumerate(parts):
        part = sources[6 * n : 6 * n + 6]
        final = last and n == len(parts) - 1
        cuts = 2 if final and len(index) % 2 == 0 else 1
        size = len(index) // cuts
        for k in range(cuts):
            some = index[k * size : (k + 1) * size]
            beside_copies(functools.partial(leave_part, some, k * size, *part, factor, staged[n]))
            if final or n < len(parts) - 1:
                ready = staged[n].at[:, :, span(k * size, size)]
                made += flush(ready, outs[-2:], sems.at[1 + n + k], half, some)
    for copy in made:
        copy.wait()


def exchange(x, axis, bit):
    return lax.ppermute(x, axis, [(i, i ^ bit) for i in range(lax.axis_size(axis))])


def crossing(x, group, step):
    return lax.ppermute(x, "ctx", [(i, i ^ (2 if (i % 2 if group is None else group) == step else 4)) for i in range(8)])


def gathered(contrib, factor, reverse):
    devices, place = lax.axis_size("ctx"), lax.axis_index("ctx")
    all_contrib = lax.all_gather(contrib, "ctx")
    all_factor = lax.all_gather(factor, "ctx")

    def lap(step, state):
        at = devices - 1 - step if reverse else step
        reached = at > place if reverse else at < place
        new = (all_factor[at][:, None, :] * state.reshape(-1, E, E)).reshape(-1, E) + all_contrib[at]
        return jnp.where(reached, new, state)

    return lax.fori_loop(0, devices, lap, jnp.zeros_like(contrib))


def summed(x):
    devices = lax.axis_size("tp")
    if devices == 1 or devices & (devices - 1):
        return lax.psum(x, "tp"), jnp.zeros_like(x)
    bit = 1
    while True:
        other = exchange(x, "tp", bit)
        bit *= 2
        if bit == devices:
            return x, other
        x = x + other


def per_device(queries, keys, values, log_decay, gain, grad_out):
    heads, tokens = log_decay.shape
    assert tokens == BLOCK and CHUNKS == 2
    features = heads * E * lax.axis_size("tp")
    fast = lax.axis_size("ctx") == 8 and heads % 16 == 0
    half = heads // 2 if fast else None
    groups = GROUPS if fast else 1
    own = (half or heads) // groups
    gain = gain[None, :]
    rows = max(16, heads)

    sides = (1, 0) if fast else (0,)
    pieces = [(g, side) for g in range(groups) for side in sides]
    late_pieces = [(g, side) for g in range(groups) for side in reversed(sides)]
    index = {(g, side): [side * (half or 0) + g * own + i for i in range(own)] for g, side in pieces}
    tall, flat, wide = (own * E, E), (BLOCK, own * E), (BLOCK, E)
    staged_shape = ((2, BLOCK, own * E), BF16)

    def at(g):
        return slice(g * own, (g + 1) * own)

    n = len(pieces)
    cum_row, rise_row, fall_row, factor, gain, *made = call(
        functools.partial(start_kernel, half, [index[piece] for piece in pieces], heads),
        [((rows, BLOCK), F32)] * 3 + [((CHUNKS + 1, rows, E), F32), (gain.shape, F32)]
        + [(flat, BF16)] * (2 * n) + [((own * E + (half or 0), E), F32), (tall, F32)],
        log_decay, gain, keys, values, anywhere=(0, 1, 2, 3),
        scratch=[pltpu.VMEM((rows, BLOCK), F32), pltpu.SemaphoreType.DMA((2 * n,)), pltpu.SemaphoreType.DMA((3,))],
    )
    whole_factor = factor[CHUNKS]
    key, value = {}, {}
    for m, piece in enumerate(pieces):
        key[piece], value[piece] = made[2 * m : 2 * m + 2]
    contrib, early = {pieces[0]: made[-2]}, {pieces[0]: made[-1]}

    def contribute(piece):
        contrib[piece], early[piece] = call(
            functools.partial(contrib_kernel, index[piece]), [(tall, F32)] * 2,
            key[piece], value[piece], fall_row, factor,
        )

    def first_step(reverse, kept, got, g, after=()):
        more = half if g == 0 and not reverse else 0
        f, h = (own_factor, other_factor) if more else (own_factor[at(g)], other_factor[at(g)])
        (chip,) = call(
            functools.partial(chip_kernel, own, reverse), [((own * E + more, E), F32)], kept, got, f, h, after=after
        )
        return kept, got, chip, crossing(chip, None if reverse else g, 0)

    def second_step(reverse, g, step, after):
        kept, got, chip, one = step
        (send,) = call(
            functools.partial(second_kernel, own, None if reverse else g, reverse), [(tall, F32)],
            one, chip, chip_factor[at(g)], factor_x[at(g)], (factor_d if g or reverse else factor_x)[at(g)], after=after,
        )
        return *step, send, crossing(send, None if reverse else g, 1)

    def last_step(reverse, g, step, after):
        kept, got, chip, one, _, two = step
        enter, send = call(
            functools.partial(enter_kernel, own, None if reverse else g, reverse), [(tall, F32)] * 2,
            one, two, factor_x[at(g)], (factor_d if g or reverse else factor_x)[at(g)], own_factor[at(g)], other_factor[at(g)], kept, got,
            after=after,
        )
        return {(g, 0): enter, (g, 1): exchange(send, "ctx", 1)}

    steps, last = [], ()
    if fast:
        gots = [exchange(contrib[0, 1], "ctx", 1)]
        contribute((0, 0))
        for g in range(1, groups):
            contribute((g, 1))
            gots.append(exchange(contrib[g, 1], "ctx", 1))
        own_factor, other_factor = whole_factor[:half], gots[0][own * E : own * E + half]
        for g in range(groups):
            if g:
                contribute((g, 0))
            steps.append(first_step(False, contrib[g, 0], gots[g], g, [contrib[groups - 1, 1]]))
        chip_factor = steps[0][2][own * E :]
        factor_x = steps[0][3][own * E :]
        factor_d = exchange(chip_factor, "ctx", 6)
        last = [step[2] for step in steps]

    cum_col, rise_col, fall_col = call(
        column_kernel, [(wide, F32)] * 3, cum_row, scratch=[pltpu.VMEM((E, BLOCK), F32)], after=last
    )
    intra, query_dec, query_dec_t, key_dec, value_dec, grad_here = {}, {}, {}, {}, {}, {}
    for piece in pieces:
        made = call(
            functools.partial(intra_kernel, half, index[piece]),
            [(flat, F32), (flat, BF16), ((own * E, BLOCK), BF16)] + [(flat, BF16)] * 3,
            grad_out, queries, key[piece], value[piece], cum_row, rise_row, cum_col, rise_col, fall_col, after=last, anywhere=(0,), scratch=[pltpu.SemaphoreType.DMA((1,))],
        )
        intra[piece], query_dec[piece], query_dec_t[piece], key_dec[piece], value_dec[piece], grad_here[piece] = made
    attended, state, sums = {}, {}, []

    def attend(piece, sums):
        attended[piece], state[piece], *sums = call(
            functools.partial(attend_kernel, half, index[piece]),
            [(flat, F32), ((CHUNKS, *tall), BF16), (wide, F32), (wide, F32)],
            query_dec[piece], intra[piece], entering[piece], early[piece], factor, grad_here[piece], gain, *sums,
        )
        return sums

    entering = {}
    if fast:
        for g in range(groups):
            steps[g] = second_step(False, g, steps[g], [intra[pieces[g]], intra[pieces[1]]])
        for g in range(groups):
            entering |= last_step(False, g, steps[g], [intra[pieces[-1]], intra[pieces[-2]], *sums])
            if g == 0:
                sums = attend((0, 0), sums)
    else:
        entering[pieces[0]] = gathered(contrib[pieces[0]], whole_factor[:heads], False)
    for piece in late_pieces:
        if piece not in attended:
            sums = attend(piece, sums)
    (sums,) = call(sum_kernel, [((8, E), F32)], *sums)
    inverse, coefficient = call(functools.partial(scale_kernel, features), [(wide, F32)] * 2, *summed(sums))

    d_attended, flow, late = {}, {}, {}

    def outer(piece, after):
        d_attended[piece], flow[piece], late[piece] = call(
            functools.partial(outer_kernel, half, index[piece]), [(flat, BF16), (tall, F32), (tall, F32)],
            inverse, coefficient, attended[piece], query_dec_t[piece], factor, grad_here[piece], gain, after=after,
        )

    steps, last = [], ()
    outer(pieces[0], ())
    if fast:
        gots = [exchange(flow[0, 1], "ctx", 1)]
        outer((0, 0), ())
        for g in range(1, groups):
            outer((g, 1), ())
            gots.append(exchange(flow[g, 1], "ctx", 1))
        for g in range(groups):
            if g:
                outer((g, 0), ())
            steps.append(first_step(True, flow[g, 0], gots[g], g, [flow[groups - 1, 1]]))
        last = [step[2] for step in steps]

    full = (queries.shape, BF16)
    sems = pltpu.SemaphoreType.DMA((2,))
    results, before, staged, intra_k, intra_v = [], None, [], {}, {}
    for piece in pieces:
        args = [
            queries, key[piece], value[piece], cum_row, cum_col, rise_col,
            d_attended[piece], state[piece], attended[piece], inverse, gain, *staged, *results,
        ]
        where = (len(args) - 2, len(args) - 1) if results else ()
        *results, intra_k[piece], intra_v[piece], out = call(
            functools.partial(back_kernel, half, index[piece], before),
            [full] * 2 + [(flat, F32)] * 2 + [staged_shape],
            *args, anywhere=where, alias=dict(zip(where, (0, 1))), outs_anywhere=2,
            scratch=[sems], after=last,
        )
        before, staged = index[piece], [out]

    def leave(group, last, before, held, aliased, targets):
        args = [factor]
        for piece in group:
            args += [value_dec[piece], key_dec[piece], intra_k[piece], intra_v[piece], leaving[piece], late[piece]]
        args += [*held, *aliased]
        where = tuple(range(len(args) - len(aliased), len(args)))
        inside = len(group) if last else len(group) - 1
        return call(
            functools.partial(
                leave_kernel, half, before, [index[piece] for piece in group], last, (len(held), len(aliased), targets)
            ),
            [full] * targets + [staged_shape] * (not last),
            *args, anywhere=where, alias={n: m for m, n in enumerate(where)}, outs_anywhere=targets,
            scratch=[pltpu.VMEM(*staged_shape)] * inside + [pltpu.SemaphoreType.DMA((2 + len(group), 2))],
        )

    leaving, tail = {}, []
    if fast:
        for g in range(groups):
            steps[g] = second_step(True, g, steps[g], [intra_k[pieces[1 + g]], *steps[0][4:5]])
        for g in range(groups):
            leaving |= last_step(True, g, steps[g], [intra_k[pieces[-1]], *tail])
            if g == 0:
                normed, grad_q, out = leave([(0, 0)], False, before, staged, results, 2)
                tail = [out]
        *results, out = leave([(0, 1), (1, 0)], False, index[0, 0], [out], [], 2)
        grad_k, grad_v = leave([(1, 1)], True, index[1, 0], [out], results, 2)
    else:
        leaving[pieces[0]] = gathered(flow[pieces[0]], whole_factor[:heads], True)
        normed, grad_q, grad_k, grad_v = leave([pieces[0]], True, before, staged, results, 4)
    return normed, grad_q, grad_k, grad_v


def solution(mesh):
    in_specs = (
        P("ctx", "tp"),
        P("ctx", "tp"),
        P("ctx", "tp"),
        P("tp", "ctx"),
        P("tp"),
        P("ctx", "tp"),
    )
    out_specs = (P("ctx", "tp"),) * 4
    return jax.shard_map(
        per_device, mesh=mesh, in_specs=in_specs, out_specs=out_specs, check_vma=False
    )
```

```python
import functools

import jax
import jax.numpy as jnp
from jax import lax
from jax.experimental import pallas as pl
from jax.experimental.pallas import tpu as pltpu
from jax.sharding import PartitionSpec as P

E = 128
BLOCK = 512
CHUNK = 256
CHUNKS = BLOCK // CHUNK
EPSILON = 1e-05
GROUPS = 2

F32 = jnp.float32
BF16 = jnp.bfloat16
IN_VMEM = pl.BlockSpec(memory_space=pltpu.VMEM)
IN_HBM = pl.BlockSpec(memory_space=pltpu.HBM)
ANY = pl.BlockSpec(memory_space=pl.ANY)
MIB = 1 << 20


def call(kernel, outs, *args, anywhere=(), after=(), outs_anywhere=0, scratch=(), alias=None, limit=20):
    args = [pltpu.with_memory_space_constraint(x, pltpu.HBM) if n in anywhere else x for n, x in enumerate(args)]
    args += after
    skip = len(after)

    def body(*refs):
        kept = len(args) - skip
        kernel(*refs[:kept], *refs[len(args) :])

    in_specs = [IN_VMEM] * (len(args) - skip) + [ANY] * skip
    for operand in anywhere:
        in_specs[operand] = IN_HBM
    return pl.pallas_call(
        body,
        out_shape=[
            (pltpu.HBM if n < outs_anywhere else pltpu.VMEM)(shape, dtype) for n, (shape, dtype) in enumerate(outs)
        ],
        in_specs=in_specs,
        out_specs=[IN_HBM] * outs_anywhere + [IN_VMEM] * (len(outs) - outs_anywhere),
        scratch_shapes=scratch,
        input_output_aliases=alias or {},
        compiler_params=pltpu.CompilerParams(vmem_limit_bytes=limit * MIB),
        cost_estimate=pl.CostEstimate(flops=0, bytes_accessed=0, transcendentals=0),
    )(*args)


def dot(a, b, contract):
    return lax.dot_general(a, b, ((contract[:1], contract[1:]), ((), ())), preferred_element_type=F32)


def beside_copies(compute):
    pl.when(lax.axis_index("ctx") >= 0)(compute)


def span(i, n=1):
    return slice(i * E, (i + n) * E)


def chunk(c):
    return slice(c * CHUNK, (c + 1) * CHUNK)


def bits(reverse=False):
    me = lax.axis_index("ctx")
    if reverse:
        me = 7 - me
    return me & 1, (me >> 1) & 1, me >> 2


def columns(half, i, n=1):
    if half is None:
        return span(i, n)
    core = lax.axis_index("ctx") & 1
    base = core if i < half else 1 - core
    return pl.ds(pl.multiple_of(base * (half * E) + (i % half) * E, E), n * E)


def head_rows(half, i, n):
    core = lax.axis_index("ctx") & 1
    base = core if i < half else 1 - core
    return pl.ds(pl.multiple_of(base * half, half), n)


def contribution(index, keys, values, fall_row, factor, contrib, early):
    decayed = []
    for n, i in enumerate(index):
        turned = keys[:, span(n)].T.astype(F32)
        decayed.append((turned * fall_row[i : i + 1, :]).astype(BF16))
    news = [
        [dot(dec[:, chunk(c)], values[chunk(c), span(n)], (1, 0)) for c in range(CHUNKS)]
        for n, dec in enumerate(decayed)
    ]
    for n, i in enumerate(index):
        early[span(n), :] = news[n][0]
        contrib[span(n), :] = factor[1, i : i + 1, :] * news[n][0] + news[n][1]


def fetch(half, pieces, sources, outs, sems):
    made = []
    for m, index in enumerate(pieces):
        cols = columns(half, index[0], len(index))
        made.append([])
        for n, source in enumerate(sources):
            k = m * len(sources) + n
            made[-1].append(pltpu.make_async_copy(source.at[:, cols], outs[k], sems.at[k]))
            made[-1][-1].start()
    return made


def start_kernel(half, pieces, heads, log_decay, gain, keys, values, *refs):
    cum_row, rise_row, fall_row, factor, gain_out = refs[:5]
    rows, sems, more = refs[-3:]
    brought, (contrib, early) = refs[5:-5], refs[-5:-3]
    rows[...] = jnp.zeros_like(rows)
    moves = [pltpu.make_async_copy(gain, gain_out, more.at[2])]
    if half is None:
        moves.append(pltpu.make_async_copy(log_decay, rows.at[0:heads, :], more.at[0]))
    else:
        for n, i in enumerate((0, half)):
            source = log_decay.at[head_rows(half, i, half), :]
            moves.append(pltpu.make_async_copy(source, rows.at[i : i + half, :], more.at[n]))
    for move in moves:
        move.start()
    made = fetch(half, pieces, (keys, values), brought, sems)
    for move in moves:
        move.wait()
    @beside_copies
    def _():
        up_to = (
            lax.broadcasted_iota(jnp.int32, (CHUNK, CHUNK), 0)
            <= lax.broadcasted_iota(jnp.int32, (CHUNK, CHUNK), 1)
        ).astype(F32).astype(BF16)
        for c in range(CHUNKS):
            whole = rows[:, chunk(c)]
            high = whole.astype(BF16)
            rest = whole - high.astype(F32)
            middle = rest.astype(BF16)
            low = (rest - middle.astype(F32)).astype(BF16)
            cum = (dot(low, up_to, (1, 0)) + dot(middle, up_to, (1, 0))) + dot(high, up_to, (1, 0))
            total = cum[:, CHUNK - 1 : CHUNK]
            cum_row[:, chunk(c)] = cum
            rise_row[:, chunk(c)] = jnp.exp(cum)
            fall_row[:, chunk(c)] = jnp.exp(total - cum)
            factor[c] = jnp.broadcast_to(jnp.exp(total), (total.shape[0], E))
        whole = factor[0] * factor[1]
        factor[CHUNKS] = whole
        if half is not None:
            contrib[len(pieces[0]) * E :, :] = factor[CHUNKS, half : 2 * half]

    for move in made[0]:
        move.wait()
    beside_copies(functools.partial(contribution, pieces[0], *brought[:2], fall_row, factor, contrib, early))
    for moves in made[1:]:
        for move in moves:
            move.wait()


def contrib_kernel(index, keys, values, fall_row, factor, contrib, early):
    contribution(index, keys, values, fall_row, factor, contrib, early)


def column_kernel(cum_row, cum_col, rise_col, fall_col, rows):
    rows[...] = jnp.zeros_like(rows)
    rows[0 : cum_row.shape[0], :] = cum_row[...]
    col = rows[...].T
    cum_col[...] = col
    rise_col[...] = jnp.exp(col)
    for c in range(CHUNKS):
        fall_col[chunk(c), :] = jnp.exp(col[(c + 1) * CHUNK - 1 : (c + 1) * CHUNK, :] - col[chunk(c)])


def chip_kernel(count, reverse, kept, got, own_factor, other_factor, sums):
    if sums.shape[0] > count * E:
        sums[count * E :, :] = own_factor[...] * other_factor[...]
    lower = bits(reverse)[0] == 0
    for n in range(count):
        mine = jnp.where(lower, other_factor[n : n + 1, :], 1.0)
        theirs = jnp.where(lower, 1.0, own_factor[n : n + 1, :])
        sums[span(n), :] = mine * kept[span(n), :] + theirs * got[span(n), :]


def second_kernel(count, group, reverse, one, own, factor, factor_x, factor_d, send):
    _, x, y = bits(reverse)
    over_x, right, later = (bits()[0] if group is None else group) == 0, x == 1, y == 1
    for n in range(count):
        f, fx, fd = factor[n : n + 1, :], factor_x[n : n + 1, :], factor_d[n : n + 1, :]
        ones = jnp.ones_like(f)
        p = jnp.where(over_x, jnp.where(right, f, 1.0), jnp.where(later, jnp.where(right, 1.0, f * fd), 0.0))
        q = jnp.where(over_x, jnp.where(right, 1.0, fx), jnp.where(later, jnp.where(right, 0.0, ones), 1.0))
        send[span(n), :] = p * one[span(n), :] + q * own[span(n), :]


def enter_kernel(count, group, reverse, one, two, factor_x, factor_d, own_factor, other_factor, kept, got, mine, send):
    core, x, y = bits(reverse)
    over_x, lower, right, later = (bits()[0] if group is None else group) == 0, core == 0, x == 1, y == 1
    for n in range(count):
        fx, fd = factor_x[n : n + 1, :], factor_d[n : n + 1, :]
        ones = jnp.ones_like(fx)
        w = jnp.where(over_x, jnp.where(right, ones, 0.0), jnp.where(later, jnp.where(right, fx, fd), 0.0))
        u = jnp.where(
            over_x,
            jnp.where(later, jnp.where(right, fx, 1.0), 0.0),
            jnp.where(later, ones, jnp.where(right, ones, 0.0)),
        )
        low = w * one[span(n), :] + u * two[span(n), :]
        f = jnp.where(lower, own_factor[n : n + 1, :], other_factor[n : n + 1, :])
        high = f * low + jnp.where(lower, kept[span(n), :], got[span(n), :])
        mine[span(n), :] = jnp.where(lower, low, high)
        send[span(n), :] = jnp.where(lower, high, low)


def intra_kernel(half, index, grad_out, queries, keys, values, cum_row, rise_row, cum_col, rise_col, fall_col, *refs):
    intra, query_dec, query_dec_t, key_dec, value_dec, grad_here, sems = refs
    made = fetch(half, [index], (grad_out,), (grad_here,), sems)
    @beside_copies
    def _():
        causal = lax.broadcasted_iota(jnp.int32, (CHUNK, CHUNK), 0) >= lax.broadcasted_iota(
            jnp.int32, (CHUNK, CHUNK), 1
        )
        scores, probs = [], []
        for n, i in enumerate(index):
            cols = columns(half, i)
            for c in range(CHUNKS):
                scores.append((n, i, c, dot(queries[chunk(c), cols], keys[chunk(c), span(n)], (1, 1))))
        for n, i, c, score in scores:
            at = chunk(c)
            spread = cum_col[at, i : i + 1] - cum_row[i : i + 1, at]
            weight = jnp.exp(jnp.where(causal, spread, -1e30))
            probs.append((n, i, c, (score * weight).astype(BF16)))
        for n, i, c, prob in probs:
            intra[chunk(c), span(n)] = dot(prob, values[chunk(c), span(n)], (1, 0))
        for n, i in enumerate(index):
            cols = columns(half, i)
            rise, fall = rise_col[:, i : i + 1], fall_col[:, i : i + 1]
            query_dec[:, span(n)] = (queries[:, cols].astype(F32) * rise).astype(BF16)
            query_dec_t[span(n), :] = (queries[:, cols].T.astype(F32) * rise_row[i : i + 1, :]).astype(BF16)
            key_dec[:, span(n)] = (keys[:, span(n)].astype(F32) * fall).astype(BF16)
            value_dec[:, span(n)] = (values[:, span(n)].astype(F32) * fall).astype(BF16)

    made[0][0].wait()


def attend_kernel(half, index, last, query_dec, intra, entering, early, factor, grad_out, gain, *refs):
    if last:
        attended, state, sums = refs[-3:]
        before = refs[:-3]
    else:
        attended, state, squares, crossed = refs[-4:]
        before = refs[:-4]
    states, inters = [], []
    for n, i in enumerate(index):
        now = entering[span(n), :]
        states.append((n, 0, now.astype(BF16)))
        states.append((n, 1, (factor[0, i : i + 1, :] * now + early[span(n), :]).astype(BF16)))
    for n, c, rounded in states:
        state[c, span(n), :] = rounded
        inters.append((n, c, dot(query_dec[chunk(c), span(n)], rounded, (1, 0))))
    totals, crosses = [0.0] * CHUNKS, [0.0] * CHUNKS
    for n, c, inter in inters:
        at, cols = chunk(c), columns(half, index[n])
        out = intra[at, span(n)] + inter
        attended[at, span(n)] = out
        totals[c] += out * out
        crosses[c] += (gain[:, cols] * grad_out[at, span(n)].astype(F32)) * out
    for c in range(CHUNKS):
        at = chunk(c)
        if before:
            totals[c], crosses[c] = totals[c] + before[0][at], crosses[c] + before[1][at]
        if not last:
            squares[at, :] = totals[c]
            crossed[at, :] = crosses[c]
    if last:
        sum_rows(totals, crosses, sums)


def sum_rows(squares, crosses, sums):
    for c in range(CHUNKS):
        for m, terms in enumerate((squares[c], crosses[c])):
            row = jnp.sum(terms.T, axis=0, keepdims=True)
            for n in range(CHUNK // E):
                at = m * (BLOCK // E) + c * (CHUNK // E) + n
                sums[at : at + 1, :] = row[:, span(n)]


def scale_kernel(features, ours, theirs, inverse, coefficient):
    sums = ours[...] + theirs[...]
    inv = lax.rsqrt(sums[0:4, :] / features + EPSILON)
    coef = inv * inv * inv * sums[4:8, :] / features
    for n in range(BLOCK // E):
        inverse[span(n), :] = jnp.broadcast_to(inv[n : n + 1, :], (E, E)).T
        coefficient[span(n), :] = jnp.broadcast_to(coef[n : n + 1, :], (E, E)).T


def outer_kernel(half, index, inverse, coefficient, attended, query_dec_t, factor, grad_out, gain, d_attended, flow, late):
    grads, news = [], []
    for n, i in enumerate(index):
        cols = columns(half, i)
        for c in range(CHUNKS):
            at = chunk(c)
            scaled = gain[:, cols] * grad_out[at, span(n)].astype(F32)
            grads.append((n, c, (inverse[at] * scaled - attended[at, span(n)] * coefficient[at]).astype(BF16)))
    for n, c, grad in grads:
        d_attended[chunk(c), span(n)] = grad
        news.append(dot(query_dec_t[span(n), chunk(c)], grad, (1, 0)))
    for n, i in enumerate(index):
        first, second = news[CHUNKS * n : CHUNKS * (n + 1)]
        late[span(n), :] = second
        flow[span(n), :] = factor[0, i : i + 1, :] * second + first


def flush(staged, outs, sems, half, index):
    made = []
    for m, out in enumerate(outs):
        cols = columns(half, index[0], len(index))
        made.append(pltpu.make_async_copy(staged.at[m], out.at[:, cols], sems.at[m]))
        made[-1].start()
    return made


def back_kernel(half, index, before, queries, keys, values, cum_row, cum_col, rise_col, d_attended, state, attended, inverse, gain, *refs):
    made = []
    if before is not None:
        made = flush(refs[0], refs[-6:-4], refs[-1], half, before)
    intra_k, intra_v, staged = refs[-4:-1]
    @beside_copies
    def _():
        causal = lax.broadcasted_iota(jnp.int32, (CHUNK, CHUNK), 0) <= lax.broadcasted_iota(
            jnp.int32, (CHUNK, CHUNK), 1
        )
        products, rounded = [], []
        for n, i in enumerate(index):
            cols = columns(half, i)
            for c in range(CHUNKS):
                at = chunk(c)
                grad = d_attended[at, span(n)]
                score = dot(keys[at, span(n)], queries[at, cols], (1, 1))
                d_prob = dot(values[at, span(n)], grad, (1, 1))
                products.append((n, i, c, score, d_prob, dot(grad, state[c, span(n), :], (1, 1))))
        for n, i, c, score, d_prob, inter in products:
            at = chunk(c)
            spread = cum_row[i : i + 1, at] - cum_col[at, i : i + 1]
            weight = jnp.exp(jnp.where(causal, spread, -1e30))
            rounded.append((n, i, c, (score * weight).astype(BF16), (d_prob * weight).astype(BF16), inter))
        for n, i, c, prob, d_score, inter in rounded:
            at, cols = chunk(c), columns(half, i)
            intra_v[at, span(n)] = dot(prob, d_attended[at, span(n)], (1, 0))
            intra_k[at, span(n)] = dot(d_score, queries[at, cols], (1, 0))
            staged[1, at, span(n)] = (dot(d_score, keys[at, span(n)], (0, 0)) + rise_col[at, i : i + 1] * inter).astype(BF16)
        for n, i in enumerate(index):
            staged[0, :, span(n)] = (gain[:, columns(half, i)] * attended[:, span(n)] * inverse[...]).astype(BF16)

    for copy in made:
        copy.wait()


def leave_part(index, start, value_dec, key_dec, intra_k, intra_v, leaving, late, factor, staged):
    flows, products = [], []
    for n, i in enumerate(index, start):
        now = leaving[span(n), :]
        flows.append((n, 1, now.astype(BF16)))
        flows.append((n, 0, (factor[1, i : i + 1, :] * now + late[span(n), :]).astype(BF16)))
    for n, c, flow in flows:
        at = chunk(c)
        products.append((n, c, dot(value_dec[at, span(n)], flow, (1, 1)), dot(key_dec[at, span(n)], flow, (1, 0))))
    for n, c, of_key, of_value in products:
        at = chunk(c)
        staged[0, at, span(n)] = (intra_k[at, span(n)] + of_key).astype(BF16)
        staged[1, at, span(n)] = (intra_v[at, span(n)] + of_value).astype(BF16)


def leave_kernel(half, before, parts, last, counts, factor, *refs):
    held, aliased, targets = counts
    sources, refs = refs[: 6 * len(parts)], refs[6 * len(parts) :]
    outs = refs[held + aliased : held + aliased + targets]
    staged, sems = refs[-1 - len(parts) : -1], refs[-1]
    if not last:
        staged = (*staged[1:], staged[0])
    made = flush(refs[0], outs[:2], sems.at[0], half, before) if held else []
    for n, index in enumerate(parts):
        part = sources[6 * n : 6 * n + 6]
        final = last and n == len(parts) - 1
        cuts = 2 if final and len(index) % 2 == 0 else 1
        size = len(index) // cuts
        for k in range(cuts):
            some = index[k * size : (k + 1) * size]
            beside_copies(functools.partial(leave_part, some, k * size, *part, factor, staged[n]))
            if final or n < len(parts) - 1:
                ready = staged[n].at[:, :, span(k * size, size)]
                made += flush(ready, outs[-2:], sems.at[1 + n + k], half, some)
    for copy in made:
        copy.wait()


def exchange(x, axis, bit):
    return lax.ppermute(x, axis, [(i, i ^ bit) for i in range(lax.axis_size(axis))])


def crossing(x, group, step):
    return lax.ppermute(x, "ctx", [(i, i ^ (2 if (i % 2 if group is None else group) == step else 4)) for i in range(8)])


def gathered(contrib, factor, reverse):
    devices, place = lax.axis_size("ctx"), lax.axis_index("ctx")
    all_contrib = lax.all_gather(contrib, "ctx")
    all_factor = lax.all_gather(factor, "ctx")

    def lap(step, state):
        at = devices - 1 - step if reverse else step
        reached = at > place if reverse else at < place
        new = (all_factor[at][:, None, :] * state.reshape(-1, E, E)).reshape(-1, E) + all_contrib[at]
        return jnp.where(reached, new, state)

    return lax.fori_loop(0, devices, lap, jnp.zeros_like(contrib))


def summed(x):
    devices = lax.axis_size("tp")
    if devices == 1 or devices & (devices - 1):
        return lax.psum(x, "tp"), jnp.zeros_like(x)
    bit = 1
    while True:
        other = exchange(x, "tp", bit)
        bit *= 2
        if bit == devices:
            return x, other
        x = x + other


def per_device(queries, keys, values, log_decay, gain, grad_out):
    heads, tokens = log_decay.shape
    assert tokens == BLOCK and CHUNKS == 2
    features = heads * E * lax.axis_size("tp")
    fast = lax.axis_size("ctx") == 8 and heads % 16 == 0
    half = heads // 2 if fast else None
    groups = GROUPS if fast else 1
    own = (half or heads) // groups
    gain = gain[None, :]
    rows = max(16, heads)

    sides = (1, 0) if fast else (0,)
    pieces = [(g, side) for g in range(groups) for side in sides]
    late_pieces = [(g, side) for g in range(groups) for side in reversed(sides)]
    index = {(g, side): [side * (half or 0) + g * own + i for i in range(own)] for g, side in pieces}
    tall, flat, wide = (own * E, E), (BLOCK, own * E), (BLOCK, E)
    staged_shape = ((2, BLOCK, own * E), BF16)

    def at(g):
        return slice(g * own, (g + 1) * own)

    n = len(pieces)
    cum_row, rise_row, fall_row, factor, gain, *made = call(
        functools.partial(start_kernel, half, [index[piece] for piece in pieces], heads),
        [((rows, BLOCK), F32)] * 3 + [((CHUNKS + 1, rows, E), F32), (gain.shape, F32)]
        + [(flat, BF16)] * (2 * n) + [((own * E + (half or 0), E), F32), (tall, F32)],
        log_decay, gain, keys, values, anywhere=(0, 1, 2, 3),
        scratch=[pltpu.VMEM((rows, BLOCK), F32), pltpu.SemaphoreType.DMA((2 * n,)), pltpu.SemaphoreType.DMA((3,))],
    )
    whole_factor = factor[CHUNKS]
    key, value = {}, {}
    for m, piece in enumerate(pieces):
        key[piece], value[piece] = made[2 * m : 2 * m + 2]
    contrib, early = {pieces[0]: made[-2]}, {pieces[0]: made[-1]}

    def contribute(piece):
        contrib[piece], early[piece] = call(
            functools.partial(contrib_kernel, index[piece]), [(tall, F32)] * 2,
            key[piece], value[piece], fall_row, factor,
        )

    def first_step(reverse, kept, got, g, after=()):
        more = half if g == 0 and not reverse else 0
        f, h = (own_factor, other_factor) if more else (own_factor[at(g)], other_factor[at(g)])
        (chip,) = call(
            functools.partial(chip_kernel, own, reverse), [((own * E + more, E), F32)], kept, got, f, h, after=after
        )
        return kept, got, chip, crossing(chip, None if reverse else g, 0)

    def second_step(reverse, g, step, after):
        kept, got, chip, one = step
        (send,) = call(
            functools.partial(second_kernel, own, None if reverse else g, reverse), [(tall, F32)],
            one, chip, chip_factor[at(g)], factor_x[at(g)], (factor_d if g or reverse else factor_x)[at(g)], after=after,
        )
        return *step, send, crossing(send, None if reverse else g, 1)

    def last_step(reverse, g, step, after):
        kept, got, chip, one, _, two = step
        enter, send = call(
            functools.partial(enter_kernel, own, None if reverse else g, reverse), [(tall, F32)] * 2,
            one, two, factor_x[at(g)], (factor_d if g or reverse else factor_x)[at(g)], own_factor[at(g)], other_factor[at(g)], kept, got,
            after=after,
        )
        return {(g, 0): enter, (g, 1): exchange(send, "ctx", 1)}

    steps, last = [], ()
    if fast:
        gots = [exchange(contrib[0, 1], "ctx", 1)]
        contribute((0, 0))
        for g in range(1, groups):
            contribute((g, 1))
            gots.append(exchange(contrib[g, 1], "ctx", 1))
        own_factor, other_factor = whole_factor[:half], gots[0][own * E : own * E + half]
        for g in range(groups):
            if g:
                contribute((g, 0))
            steps.append(first_step(False, contrib[g, 0], gots[g], g, [contrib[groups - 1, 1]]))
        chip_factor = steps[0][2][own * E :]
        factor_x = steps[0][3][own * E :]
        factor_d = exchange(chip_factor, "ctx", 6)
        last = [step[2] for step in steps]

    cum_col, rise_col, fall_col = call(
        column_kernel, [(wide, F32)] * 3, cum_row, scratch=[pltpu.VMEM((E, BLOCK), F32)], after=last
    )
    intra, query_dec, query_dec_t, key_dec, value_dec, grad_here = {}, {}, {}, {}, {}, {}
    for piece in pieces:
        made = call(
            functools.partial(intra_kernel, half, index[piece]),
            [(flat, F32), (flat, BF16), ((own * E, BLOCK), BF16)] + [(flat, BF16)] * 3,
            grad_out, queries, key[piece], value[piece], cum_row, rise_row, cum_col, rise_col, fall_col, after=last, anywhere=(0,), scratch=[pltpu.SemaphoreType.DMA((1,))],
        )
        intra[piece], query_dec[piece], query_dec_t[piece], key_dec[piece], value_dec[piece], grad_here[piece] = made
    attended, state, sums = {}, {}, []

    def attend(piece, sums):
        attended[piece], state[piece], *sums = call(
            functools.partial(attend_kernel, half, index[piece], piece == late_pieces[-1]),
            [(flat, F32), ((CHUNKS, *tall), BF16)]
            + ([((8, E), F32)] if piece == late_pieces[-1] else [(wide, F32)] * 2),
            query_dec[piece], intra[piece], entering[piece], early[piece], factor, grad_here[piece], gain, *sums,
        )
        return sums

    entering = {}
    if fast:
        for g in range(groups):
            steps[g] = second_step(False, g, steps[g], [intra[pieces[g]], intra[pieces[1]]])
        for g in range(groups):
            entering |= last_step(False, g, steps[g], [intra[pieces[-1]], intra[pieces[-2]], *sums])
            if g == 0:
                sums = attend((0, 0), sums)
    else:
        entering[pieces[0]] = gathered(contrib[pieces[0]], whole_factor[:heads], False)
    for piece in late_pieces:
        if piece not in attended:
            sums = attend(piece, sums)
    (sums,) = sums
    inverse, coefficient = call(functools.partial(scale_kernel, features), [(wide, F32)] * 2, *summed(sums))

    d_attended, flow, late = {}, {}, {}

    def outer(piece, after):
        d_attended[piece], flow[piece], late[piece] = call(
            functools.partial(outer_kernel, half, index[piece]), [(flat, BF16), (tall, F32), (tall, F32)],
            inverse, coefficient, attended[piece], query_dec_t[piece], factor, grad_here[piece], gain, after=after,
        )

    steps, last = [], ()
    outer(pieces[0], ())
    if fast:
        gots = [exchange(flow[0, 1], "ctx", 1)]
        outer((0, 0), ())
        for g in range(1, groups):
            outer((g, 1), ())
            gots.append(exchange(flow[g, 1], "ctx", 1))
        for g in range(groups):
            if g:
                outer((g, 0), ())
            steps.append(first_step(True, flow[g, 0], gots[g], g))
        last = [step[2] for step in steps]

    full = (queries.shape, BF16)
    sems = pltpu.SemaphoreType.DMA((2,))
    results, before, staged, intra_k, intra_v = [], None, [], {}, {}
    for piece in pieces:
        args = [
            queries, key[piece], value[piece], cum_row, cum_col, rise_col,
            d_attended[piece], state[piece], attended[piece], inverse, gain, *staged, *results,
        ]
        where = (len(args) - 2, len(args) - 1) if results else ()
        *results, intra_k[piece], intra_v[piece], out = call(
            functools.partial(back_kernel, half, index[piece], before),
            [full] * 2 + [(flat, F32)] * 2 + [staged_shape],
            *args, anywhere=where, alias=dict(zip(where, (0, 1))), outs_anywhere=2,
            scratch=[sems], after=last,
        )
        before, staged = index[piece], [out]

    def leave(group, last, before, held, aliased, targets):
        args = [factor]
        for piece in group:
            args += [value_dec[piece], key_dec[piece], intra_k[piece], intra_v[piece], leaving[piece], late[piece]]
        args += [*held, *aliased]
        where = tuple(range(len(args) - len(aliased), len(args)))
        inside = len(group) if last else len(group) - 1
        return call(
            functools.partial(
                leave_kernel, half, before, [index[piece] for piece in group], last, (len(held), len(aliased), targets)
            ),
            [full] * targets + [staged_shape] * (not last),
            *args, anywhere=where, alias={n: m for m, n in enumerate(where)}, outs_anywhere=targets,
            scratch=[pltpu.VMEM(*staged_shape)] * inside + [pltpu.SemaphoreType.DMA((2 + len(group), 2))],
        )

    leaving, tail = {}, []
    if fast:
        for g in range(groups):
            steps[g] = second_step(True, g, steps[g], [intra_k[pieces[1 + g]], *steps[0][4:5]])
        for g in range(groups):
            leaving |= last_step(True, g, steps[g], [intra_k[pieces[-1]], *tail])
            if g == 0:
                normed, grad_q, out = leave([(0, 0)], False, before, staged, results, 2)
                tail = [out]
        *results, out = leave([(0, 1), (1, 0)], False, index[0, 0], [out], [], 2)
        grad_k, grad_v = leave([(1, 1)], True, index[1, 0], [out], results, 2)
    else:
        leaving[pieces[0]] = gathered(flow[pieces[0]], whole_factor[:heads], True)
        normed, grad_q, grad_k, grad_v = leave([pieces[0]], True, before, staged, results, 4)
    return normed, grad_q, grad_k, grad_v


def solution(mesh):
    in_specs = (
        P("ctx", "tp"),
        P("ctx", "tp"),
        P("ctx", "tp"),
        P("tp", "ctx"),
        P("tp"),
        P("ctx", "tp"),
    )
    out_specs = (P("ctx", "tp"),) * 4
    return jax.shard_map(
        per_device, mesh=mesh, in_specs=in_specs, out_specs=out_specs, check_vma=False
    )
```
